256 devices in a mesh: seq: 16 (over y, x_lo, core), expert: 16 (over z, x_hi).
Axes of the slice: x: 4 (x_hi: 2, x_lo: 2; x = x_hi * 2 + x_lo), y: 4, z: 8, core: 2. Of those that a mesh axis runs over, the one named last changes fastest.
Arguments:
- tokens: bfloat16 [16, 16384, 1280], P('expert', 'seq'), may hold values from -40 to 40
- slot_params: bfloat16 [1280, 128], P(None, 'expert'), may hold values from -6.1 to 6.1
- up_weight: bfloat16 [128, 1280, 2560], P('expert', None, 'seq'), may hold values from -0.625 to 0.625
- down_weight: bfloat16 [128, 2560, 1280], P('expert', 'seq'), may hold values from -0.125 to 0.125
Outputs:
- mixed: bfloat16 [16, 16384, 1280], P('expert', 'seq')
The draws below stay inside these ranges and needn't reach their ends.
All inputs are finite; a program needn't handle non-finite values.
Results may differ from the reference program's by a relative error of at most 0.0071.
Values may be sent and summed in bfloat16 or wider, within the bound.
A program may use at most 64 MiB of HBM per device.

```python
import math
import jax
import jax.numpy as jnp
from jax import lax

D = 1280
FF = 2560
EXPERTS = 128
PATCHES = 16384
CLIPS = 16


def draw_tokens(key, part):
    key = jax.random.fold_in(key, 11)
    values = jax.random.normal(key, (CLIPS, PATCHES, D), jnp.float32)
    return jnp.clip(values, -6.0, 6.0).astype(jnp.bfloat16)


def draw_slot_params(key, part):
    key = jax.random.fold_in(key, 23)
    values = jnp.clip(jax.random.normal(key, (D, EXPERTS), jnp.float32), -4.0, 4.0)
    return (values * (3.0 / math.sqrt(D))).astype(jnp.bfloat16)


def shard_levels(key, dims, cuts, low, top_value):
    factor_of, own = 1.0, jax.random.fold_in(key, 6)
    for axis_at, parts in cuts:
        heights = jnp.exp(jax.random.uniform(jax.random.fold_in(own, axis_at), (parts,), jnp.float32, low / len(cuts), top_value / len(cuts)))
        factor_of = factor_of * jnp.repeat(heights, dims[axis_at] // parts).reshape([-1 if axis == axis_at else 1 for axis in range(len(dims))])
    return factor_of


def normal_values(stream_key, dims, spread, limit, pieces=(), held_as=jnp.bfloat16):
    entries = spread * jax.random.normal(stream_key, dims, jnp.float32)
    if pieces:
        entries = entries * shard_levels(stream_key, dims, pieces, -0.22, 0.18)
    return jnp.clip(entries, -limit, limit).astype(held_as)


def setup_inputs(seed: int = 0) -> dict:
    splits = jax.random.split(jax.random.key(seed), 5)
    return {
        "tokens": draw_tokens(jax.random.fold_in(splits[4], 71), 0),
        "slot_params": draw_slot_params(jax.random.fold_in(splits[4], 71), 0),
        "up_weight": normal_values(splits[2], (EXPERTS, D, FF), (D // 16) ** -0.5, 0.625, ((0, 16), (2, 16))),
        "down_weight": normal_values(splits[3], (EXPERTS, FF, D), FF ** -0.5, 0.125, ((0, 16), (1, 16))),
    }


def clip_inputs(rows, slot_params):
    logits = jnp.dot(rows, slot_params, preferred_element_type=jnp.float32)
    top = jnp.max(logits, axis=0)
    scaled = jnp.exp(logits - top[None, :])
    totals = jnp.sum(scaled, axis=0)
    weights = scaled.astype(jnp.bfloat16)
    gathered = jnp.dot(weights.T, rows, preferred_element_type=jnp.float32)
    return (gathered / totals[:, None]).astype(jnp.bfloat16)


def expert_apply(packed):
    inputs, first, second = packed
    inner = jnp.dot(inputs, first, preferred_element_type=jnp.float32)
    hidden = jax.nn.gelu(inner, approximate=False).astype(jnp.bfloat16)
    return jnp.dot(hidden, second, preferred_element_type=jnp.float32).astype(jnp.bfloat16)


def reference(tokens, slot_params, up_weight, down_weight):
    slot_in = lax.map(lambda rows: clip_inputs(rows, slot_params), tokens)
    by_expert = jnp.transpose(slot_in, (1, 0, 2))
    slot_out = lax.map(expert_apply, (by_expert, up_weight, down_weight))
    slot_out = jnp.transpose(slot_out, (1, 0, 2))

    def combine(packed):
        rows, outputs = packed
        logits = jnp.dot(rows, slot_params, preferred_element_type=jnp.float32)
        peak = jnp.max(logits, axis=1)
        expo = jnp.exp(logits - peak[:, None])
        mix_weights = (expo / jnp.sum(expo, axis=1)[:, None]).astype(jnp.bfloat16)
        return jnp.dot(mix_weights, outputs, preferred_element_type=jnp.float32).astype(jnp.bfloat16)

    return lax.map(combine, (tokens, slot_out))
```

```python
import jax
import jax.numpy as jnp
from jax import lax
from jax.experimental import pallas as pl
from jax.experimental.pallas import tpu as pltpu
from jax.sharding import PartitionSpec as P

MESH = pl.DeviceIdType.MESH
BF = jnp.bfloat16
F32 = jnp.float32
NE = 16
NC = 8
K = 8
HALF = 640
ROWS = 1024
FD = 160
SLOTS = NE * K

EXP_ORDER = (7, 9, 8, 5, 11, 6, 10, 3, 13, 4, 12, 1, 15, 2, 14)
EXP_NEAR = tuple(reversed(EXP_ORDER))
CHIP_ORDER = (3, 5, 4, 1, 7, 2, 6)
CHIP_NEAR = (0, 2, 6, 1, 7, 4, 3, 5)


def nt(a, b):
    return lax.dot_general(a, b, (((1,), (1,)), ((), ())), preferred_element_type=F32)


def mm(a, b):
    return jnp.dot(a, b, preferred_element_type=F32)


def gelu(v):
    return 0.5 * v * (1.0 + lax.erf(v * 0.7071067811865476))


def kernel(
    tok_hbm, sp_hbm, up_hbm, dn_hbm, out_ref,
    tokh, upv, dnv, tab, lg, wt, xs, stat, pst, cst, fin, ft,
    psend, pown, precv, rs_send, rs_recv, a_send, a_recv, xb,
    po_send, po_own, po_recv, ro_send, ro_recv, b_send, b_recv, ret, mxs, mw,
    load_sem, tab_s, tab_r, tabf_s, tabf_r, pst_s, pst_r, cst_s, cst_r, pp_s, pp_r,
    rs_s, rs_r, a_s, a_r, xg_s, xg_r, xf_s, xf_r, po_s, po_r, ro_s, ro_r, b_s, b_r,
    rg_s, rg_r, rf_s, rf_r,
):
    s = lax.axis_index("seq")
    e = lax.axis_index("expert")
    chip = lax.div(s, 2)
    h = lax.rem(s, 2)
    o = 1 - h
    sib = (chip * 2 + o, e)

    def chip_at(j):
        return lax.rem(chip + j, NC)

    def chip_dev(j):
        return (chip_at(j) * 2 + h, e)

    def exp_at(i):
        return lax.rem(e + i, NE)

    def copy(src, dst, ssem, rsem, dev):
        return pltpu.make_async_remote_copy(
            src_ref=src, dst_ref=dst, send_sem=ssem, recv_sem=rsem, device_id=dev, device_id_type=MESH
        )

    own = pltpu.make_async_copy(sp_hbm.at[:, pl.ds(0, HALF)], tab.at[0, e], load_sem.at[0])
    own1 = pltpu.make_async_copy(sp_hbm.at[:, pl.ds(HALF, HALF)], tab.at[1, e], load_sem.at[1])
    own.start()
    own1.start()
    loads = []
    for a, (src, dst) in enumerate(((tok_hbm, tokh), (up_hbm, upv), (dn_hbm, dnv))):
        for half in range(2):
            lanes = pl.ds(half * HALF, HALF)
            view = src.at[:, lanes] if a == 0 else src.at[:, :, lanes]
            c = pltpu.make_async_copy(view, dst.at[half], load_sem.at[2 + 2 * a + half])
            c.start()
            loads.append(c)

    barrier = pltpu.get_barrier_semaphore()
    for i in EXP_ORDER:
        pl.semaphore_signal(barrier, inc=1, device_id=(s, exp_at(i)), device_id_type=MESH)
    for j in CHIP_ORDER:
        pl.semaphore_signal(barrier, inc=1, device_id=chip_dev(j), device_id_type=MESH)
    pl.semaphore_signal(barrier, inc=1, device_id=sib, device_id_type=MESH)
    own.wait()
    own1.wait()
    pl.semaphore_wait(barrier, NE - 1 + NC - 1 + 1)

    sends = []
    for i in EXP_ORDER:
        c = copy(tab.at[h, e], tab.at[h, e], tab_s.at[i], tab_r.at[i], (s, exp_at(i)))
        c.start()
        sends.append(c)
    fin[...] = jnp.zeros_like(fin)
    for i in EXP_NEAR:
        src = tab.at[h, exp_at(NE - i)]
        copy(src, src, tab_s.at[i], tab_r.at[i], (s, exp_at(i))).wait_recv()
        c = copy(src, src, tabf_s.at[i], tabf_r.at[i], sib)
        c.start()
        sends.append(c)
    loads[0].wait()
    loads[1].wait()
    half_table = tab[h].astype(F32).reshape(SLOTS, HALF).astype(BF)
    for n in range(4):
        part = pl.ds(n * 256, 256)
        lg[:, part] = nt(half_table, tokh[h, part, :])
    for i in EXP_NEAR:
        src = tab.at[o, exp_at(NE - i)]
        copy(src, src, tabf_s.at[i], tabf_r.at[i], sib).wait_recv()
    half_table = tab[o].astype(F32).reshape(SLOTS, HALF).astype(BF)
    for n in range(4):
        part = pl.ds(n * 256, 256)
        lg[:, part] += nt(half_table, tokh[o, part, :])

    lane = lax.broadcasted_iota(jnp.int32, (32, 128), 1)
    for r in range(0, SLOTS, 32):
        part = pl.ds(r, 32)
        v = lg[part, :]
        m = jnp.max(v, axis=1, keepdims=True)
        ex = jnp.exp(v - m)
        l = jnp.sum(ex, axis=1, keepdims=True)
        wt[part, :] = ex.astype(BF)
        xs[part, :] = jnp.where(lane < 64, m, l)
    xt = xs[...].T
    m0 = jnp.broadcast_to(xt[0:1, :], (8, 128))
    l0 = jnp.broadcast_to(xt[64:65, :], (8, 128))
    stat[0] = m0
    stat[1] = l0
    c_pst = copy(stat, pst, pst_s, pst_r, sib)
    c_pst.start()

    psend[...] = mm(wt[...], tokh[o])
    c_pst.wait_recv()
    m1 = pst[0]
    mc = jnp.maximum(m0, m1)
    g0 = jnp.exp(m0 - mc)
    cst[0, 0] = mc
    cst[0, 1] = l0 * g0 + pst[1] * jnp.exp(m1 - mc)
    c_cst = []
    for j in CHIP_ORDER:
        c = copy(cst.at[0], cst.at[j], cst_s.at[j], cst_r.at[j], chip_dev(j))
        c.start()
        c_cst.append(c)
    scale = jnp.broadcast_to(g0[0:1, :], (128, 128)).T
    for n in range(5):
        part = pl.ds(n * 128, 128)
        psend[:, part] = psend[:, part] * scale
    c_pp = copy(psend, precv, pp_s, pp_r, sib)
    c_pp.start()
    sums = mm(wt[...], tokh[h])
    for n in range(5):
        pown[n] = sums[:, n * 128 : n * 128 + 128] * scale
    c_pp.wait_recv()
    for n in range(5):
        part = pl.ds(n * 128, 128)
        pown[n] = pown[n] + precv[:, part]
        for k in range(K):
            rs_send[k, :, part] = pown[n, pl.ds(k, NE, stride=K), :].astype(BF)
    c_rs = []
    for j in CHIP_ORDER:
        c = copy(rs_send.at[chip_at(j)], rs_recv.at[j], rs_s.at[j], rs_r.at[j], chip_dev(j))
        c.start()
        c_rs.append(c)

    for n in range(4):
        part = pl.ds(n * 256, 256)
        v = lg[:, part]
        ex = jnp.exp(v - jnp.max(v, axis=0, keepdims=True))
        ex = ex / jnp.sum(ex, axis=0, keepdims=True)
        mxs[2 * n] = ex[:, :128]
        mxs[2 * n + 1] = ex[:, 128:]
    for n in range(8):
        part = pl.ds(n * 128, 128)
        rows = [mxs[n, pl.ds(k, NE, stride=K), :] for k in range(K)]
        mw[part, :] = jnp.concatenate(rows, axis=0).T.astype(BF)

    for c in c_cst:
        c.wait_recv()
    top = cst[0, 0]
    for j in range(1, NC):
        top = jnp.maximum(top, cst[j, 0])
    total = jnp.zeros((8, 128), F32)
    for j in range(NC):
        total += cst[j, 1] * jnp.exp(cst[j, 0] - top)
    row = lax.broadcasted_iota(jnp.int32, (8, 128), 0)
    factors = jnp.zeros((8, 128), F32)
    for j in range(NC):
        factors = jnp.where(row == j, jnp.exp(cst[j, 0] - top) / total, factors)
    fin[0:8, :] = factors
    ft[...] = fin[...].T
    fk = ft[pl.ds(chip, NE, stride=K), :]

    y = rs_send[chip].astype(F32) * fk[:, 0:1]
    for c in sends:
        c.wait_send()
    c_pst.wait_send()
    c_pp.wait_send()
    for c in c_cst:
        c.wait_send()
    for j in CHIP_NEAR[1:]:
        copy(rs_recv.at[j], rs_recv.at[j], rs_s.at[j], rs_r.at[j], chip_dev(j)).wait_recv()
        y += rs_recv[j].astype(F32) * fk[:, j : j + 1]

    def rows_across(value, send, recv, ssem, rsem):
        send[...] = value.reshape(NE, 1, HALF)
        started = []
        for i in EXP_ORDER:
            c = copy(send.at[exp_at(i)], recv.at[e], ssem.at[i], rsem.at[i], (s, exp_at(i)))
            c.start()
            started.append(c)
        recv[e] = send[e]
        for i in EXP_NEAR:
            dst = recv.at[exp_at(NE - i)]
            copy(dst, dst, ssem.at[i], rsem.at[i], (s, exp_at(i))).wait_recv()
        return recv[...].reshape(NE, HALF), started

    def spread(value, buf, gs, gr, fs, fr):
        buf[h, chip] = value
        started = []
        for j in CHIP_ORDER:
            c = copy(buf.at[h, chip], buf.at[h, chip], gs.at[j], gr.at[j], chip_dev(j))
            c.start()
            started.append(c)
        c = copy(buf.at[h, chip], buf.at[h, chip], fs.at[0], fr.at[0], sib)
        c.start()
        started.append(c)
        return started

    def forward(j, buf, gs, gr, fs, fr, started):
        src = buf.at[h, chip_at(NC - j)]
        copy(src, src, gs.at[j], gr.at[j], chip_dev(j)).wait_recv()
        c = copy(src, src, fs.at[j], fr.at[j], sib)
        c.start()
        started.append(c)

    def other_half(j, buf, fs, fr):
        src = buf.at[o, chip_at(NC - j)]
        copy(src, src, fs.at[j], fr.at[j], sib).wait_recv()

    x_own, c_a = rows_across(y, a_send, a_recv, a_s, a_r)
    c_xg = spread(x_own.astype(BF), xb, xg_s, xg_r, xf_s, xf_r)
    for c in c_rs:
        c.wait_send()
    for c in c_a:
        c.wait_send()
    for c in loads[2:]:
        c.wait()

    c_po = []
    c_ro = []

    def expert(j):
        k = chip_at(NC - j)
        inner = nt(xb[h, k], upv[h, k])
        other_half(j, xb, xf_s, xf_r)
        inner += nt(xb[o, k], upv[o, k])
        hidden = gelu(inner).astype(BF)
        po_send[j] = mm(hidden, dnv[o, k])
        c = copy(po_send.at[j], po_recv.at[j], po_s.at[j], po_r.at[j], sib)
        c.start()
        c_po.append(c)
        po_own[j] = mm(hidden, dnv[h, k])

    def reduce_on(j):
        copy(po_send.at[j], po_recv.at[j], po_s.at[j], po_r.at[j], sib).wait_recv()
        po_own[j] = po_own[j] + po_recv[j]
        if j:
            ro_send[j] = po_own[j].astype(BF)
            c = copy(ro_send.at[j], ro_recv.at[j], ro_s.at[j], ro_r.at[j], chip_dev(NC - j))
            c.start()
            c_ro.append(c)

    for n in range(1, 3):
        forward(CHIP_NEAR[n], xb, xg_s, xg_r, xf_s, xf_r, c_xg)
    for n in range(NC):
        expert(CHIP_NEAR[n])
        if n + 3 < NC:
            forward(CHIP_NEAR[n + 3], xb, xg_s, xg_r, xf_s, xf_r, c_xg)
        if n:
            reduce_on(CHIP_NEAR[n - 1])
    reduce_on(CHIP_NEAR[NC - 1])
    y = po_own[0]
    for c in c_xg + c_po:
        c.wait_send()
    for j in CHIP_NEAR[1:]:
        copy(ro_recv.at[j], ro_recv.at[j], ro_s.at[j], ro_r.at[j], chip_dev(j)).wait_recv()
        y += ro_recv[j].astype(F32)

    r_own, c_b = rows_across(y, b_send, b_recv, b_s, b_r)
    c_rg = spread(r_own.astype(BF), ret, rg_s, rg_r, rf_s, rf_r)
    for c in c_ro + c_b:
        c.wait_send()
    for j in CHIP_NEAR[1:]:
        forward(j, ret, rg_s, rg_r, rf_s, rf_r, c_rg)

    def mix(half):
        table = ret[half].reshape(SLOTS, HALF)
        lanes = pl.ds(pl.multiple_of(half * HALF, 128), HALF)
        for n in range(4):
            part = pl.ds(n * 256, 256)
            out_ref[part, lanes] = mm(mw[part, :], table).astype(BF)

    mix(h)
    for j in CHIP_NEAR:
        other_half(j, ret, rf_s, rf_r)
    mix(o)
    for c in c_rg:
        c.wait_send()


def shards(tokens, slot_params, up_weight, down_weight):
    vm = pltpu.VMEM
    dma = pltpu.SemaphoreType.DMA
    call = pl.pallas_call(
        kernel,
        out_shape=jax.ShapeDtypeStruct((ROWS, 2 * HALF), BF),
        in_specs=[pl.BlockSpec(memory_space=pl.ANY)] * 4,
        out_specs=pl.BlockSpec(memory_space=pltpu.VMEM),
        scratch_shapes=[
            vm((2, ROWS, HALF), BF),
            vm((2, K, FD, HALF), BF),
            vm((2, K, FD, HALF), BF),
            vm((2, NE, K, HALF), BF),
            vm((SLOTS, ROWS), F32),
            vm((SLOTS, ROWS), BF),
            vm((SLOTS, 128), F32),
            vm((2, 8, 128), F32),
            vm((2, 8, 128), F32),
            vm((NC, 2, 8, 128), F32),
            vm((128, 128), F32),
            vm((128, 128), F32),
            vm((SLOTS, HALF), F32),
            vm((5, SLOTS, 128), F32),
            vm((SLOTS, HALF), F32),
            vm((NC, NE, HALF), BF),
            vm((NC, NE, HALF), BF),
            vm((NE, 1, HALF), F32),
            vm((NE, 1, HALF), F32),
            vm((2, NC, NE, HALF), BF),
            vm((NC, NE, HALF), F32),
            vm((NC, NE, HALF), F32),
            vm((NC, NE, HALF), F32),
            vm((NC, NE, HALF), BF),
            vm((NC, NE, HALF), BF),
            vm((NE, 1, HALF), F32),
            vm((NE, 1, HALF), F32),
            vm((2, NC, NE, HALF), BF),
            vm((8, SLOTS, 128), F32),
            vm((ROWS, SLOTS), BF),
            dma((8,)),
            dma((NE,)), dma((NE,)), dma((NE,)), dma((NE,)),
            dma, dma,
            dma((NC,)), dma((NC,)),
            dma, dma,
            dma((NC,)), dma((NC,)),
            dma((NE,)), dma((NE,)),
            dma((NC,)), dma((NC,)), dma((NC,)), dma((NC,)),
            dma((NC,)), dma((NC,)),
            dma((NC,)), dma((NC,)),
            dma((NE,)), dma((NE,)),
            dma((NC,)), dma((NC,)), dma((NC,)), dma((NC,)),
        ],
        compiler_params=pltpu.CompilerParams(
            collective_id=0, has_side_effects=True, vmem_limit_bytes=48 * 2**20
        ),
        cost_estimate=pl.CostEstimate(flops=1_400_000_000, bytes_accessed=14_000_000, transcendentals=400_000),
        name="soft_moe",
    )
    mixed = call(
        tokens.reshape(ROWS, 2 * HALF),
        slot_params.T,
        jnp.transpose(up_weight, (0, 2, 1)),
        down_weight,
    )
    return mixed.reshape(tokens.shape)


def solution(mesh):
    in_specs = (
        P("expert", "seq", None),
        P(None, "expert"),
        P("expert", None, "seq"),
        P("expert", "seq", None),
    )
    out_specs = P("expert", "seq", None)
    return jax.shard_map(shards, mesh=mesh, in_specs=in_specs, out_specs=out_specs, check_vma=False)
```

```python
import jax
import jax.numpy as jnp
from jax import lax
from jax.experimental import pallas as pl
from jax.experimental.pallas import tpu as pltpu
from jax.sharding import PartitionSpec as P

MESH = pl.DeviceIdType.MESH
BF = jnp.bfloat16
F32 = jnp.float32
NE = 16
NZ = 8
NC = 8
K = 8
HALF = 640
ROWS = 1024
FD = 160
SLOTS = NE * K

EXP_FAR = (
    (1, 4), (1, 3), (1, 5), (0, 4), (1, 2), (1, 6), (0, 3), (0, 5),
    (1, 1), (1, 7), (0, 2), (0, 6), (1, 0), (0, 1), (0, 7),
)
EXP_NEAR = tuple(reversed(EXP_FAR))
CHIP_FAR = ((2, 1), (2, 0), (1, 1), (3, 1), (1, 0), (3, 0), (0, 1))
CHIP_NEAR = tuple(reversed(CHIP_FAR))


def nt(a, b):
    return lax.dot_general(a, b, (((1,), (1,)), ((), ())), preferred_element_type=F32)


def mm(a, b):
    return jnp.dot(a, b, preferred_element_type=F32)


def gelu(v):
    return 0.5 * v * (1.0 + lax.erf(v * 0.7071067811865476))


def kernel(
    tok_hbm, sp_hbm, up_hbm, dn_hbm, out_ref,
    tokh, upv, dnv, tab, lg, wt, xs, stat, pst, cst, fin, ft,
    psend, pown, precv, rs_send, rs_recv, a_send, a_recv, xb,
    po_send, po_own, po_recv, ro_send, ro_recv, b_send, b_recv, ret, mxs, mw,
    load_sem, tab_s, tab_r, tabf_s, tabf_r, pst_s, pst_r, cst_s, cst_r, pp_s, pp_r,
    rs_s, rs_r, a_s, a_r, xg_s, xg_r, xf_s, xf_r, po_s, po_r, ro_s, ro_r, b_s, b_r,
    rg_s, rg_r, rf_s, rf_r,
):
    s = lax.axis_index("seq")
    e = lax.axis_index("expert")
    chip = lax.div(s, 2)
    h = lax.rem(s, 2)
    o = 1 - h
    y = lax.div(chip, 2)
    x_lo = lax.rem(chip, 2)
    z = lax.div(e, 2)
    x_hi = lax.rem(e, 2)
    sib = (chip * 2 + o, e)
    flipped = y * 2 + 1 - x_lo

    def chip_at(p):
        return lax.rem(y + p[0], 4) * 2 + (1 - x_lo if p[1] else x_lo)

    def chip_from(p):
        return chip_at((4 - p[0], p[1]))

    def chip_dev(p):
        return (chip_at(p) * 2 + h, e)

    def exp_at(i):
        return lax.rem(z + i[1], NZ) * 2 + (1 - x_hi if i[0] else x_hi)

    def exp_from(i):
        return exp_at((i[0], NZ - i[1]))

    def exp_dev(i):
        return ((flipped if i[0] else chip) * 2 + h, exp_at(i))

    def cid(p):
        return p[0] * 2 + p[1]

    def eid(i):
        return i[0] * NZ + i[1]

    live = []

    def drain(count=None):
        for c in live[:count]:
            c.wait_send()
        del live[:count]

    def copy(src, dst, ssem, rsem, dev):
        return pltpu.make_async_remote_copy(
            src_ref=src, dst_ref=dst, send_sem=ssem, recv_sem=rsem, device_id=dev, device_id_type=MESH
        )

    def send(src, dst, ssem, rsem, dev):
        c = copy(src, dst, ssem, rsem, dev)
        c.start()
        live.append(c)

    def arrived(dst, ssem, rsem):
        copy(dst, dst, ssem, rsem, sib).wait_recv()

    barrier = pltpu.get_barrier_semaphore()
    for i in EXP_FAR:
        pl.semaphore_signal(barrier, inc=1, device_id=exp_dev(i), device_id_type=MESH)
    for p in CHIP_FAR:
        pl.semaphore_signal(barrier, inc=1, device_id=chip_dev(p), device_id_type=MESH)
    pl.semaphore_signal(barrier, inc=1, device_id=sib, device_id_type=MESH)

    loads = []
    for half in range(2):
        lanes = pl.ds(half * HALF, HALF)
        c = pltpu.make_async_copy(sp_hbm.at[:, lanes], tab.at[half, e], load_sem.at[6 + half])
        c.start()
        loads.append(c)
    for a, (src, dst) in enumerate(((tok_hbm, tokh), (up_hbm, upv), (dn_hbm, dnv))):
        for half in range(2):
            lanes = pl.ds(half * HALF, HALF)
            view = src.at[:, lanes] if a == 0 else src.at[:, :, lanes]
            c = pltpu.make_async_copy(view, dst.at[half], load_sem.at[2 * a + half])
            c.start()
            loads.append(c)
    fin[...] = jnp.zeros_like(fin)
    loads[0].wait()
    loads[1].wait()
    pl.semaphore_wait(barrier, NE - 1 + NC - 1 + 1)

    for i in EXP_FAR:
        send(tab.at[h, e], tab.at[h, e], tab_s.at[eid(i)], tab_r.at[eid(i)], exp_dev(i))
    for i in EXP_NEAR:
        src = tab.at[h, exp_from(i)]
        arrived(src, tab_s.at[eid(i)], tab_r.at[eid(i)])
        send(src, src, tabf_s.at[eid(i)], tabf_r.at[eid(i)], sib)
    loads[2].wait()
    loads[3].wait()
    half_table = tab[h].astype(F32).reshape(SLOTS, HALF).astype(BF)
    for n in range(4):
        part = pl.ds(n * 256, 256)
        lg[:, part] = nt(half_table, tokh[h, part, :])
    for i in EXP_NEAR:
        arrived(tab.at[o, exp_from(i)], tabf_s.at[eid(i)], tabf_r.at[eid(i)])
    half_table = tab[o].astype(F32).reshape(SLOTS, HALF).astype(BF)
    for n in range(4):
        part = pl.ds(n * 256, 256)
        lg[:, part] += nt(half_table, tokh[o, part, :])

    lane = lax.broadcasted_iota(jnp.int32, (32, 128), 1)
    for r in range(0, SLOTS, 32):
        part = pl.ds(r, 32)
        v = lg[part, :]
        m = jnp.max(v, axis=1, keepdims=True)
        ex = jnp.exp(v - m)
        l = jnp.sum(ex, axis=1, keepdims=True)
        wt[part, :] = ex.astype(BF)
        xs[part, :] = jnp.where(lane < 64, m, l)
    xt = xs[...].T
    m0 = jnp.broadcast_to(xt[0:1, :], (8, 128))
    l0 = jnp.broadcast_to(xt[64:65, :], (8, 128))
    stat[0] = m0
    stat[1] = l0
    send(stat, pst, pst_s, pst_r, sib)

    for n, w in ((0, 2), (2, 2), (4, 1)):
        sums = mm(wt[...], tokh[o, :, pl.ds(n * 128, w * 128)])
        for q in range(w):
            psend[n + q] = sums[:, q * 128 : q * 128 + 128]
        part = pl.ds(n, w)
        send(psend.at[part], precv.at[part], pp_s.at[n], pp_r.at[n], sib)
    sums = mm(wt[...], tokh[h])
    for n in range(5):
        pown[n] = sums[:, n * 128 : n * 128 + 128]
    arrived(pst, pst_s, pst_r)
    m1 = pst[0]
    mc = jnp.maximum(m0, m1)
    g0 = jnp.exp(m0 - mc)
    g1 = jnp.exp(m1 - mc)
    cst[0, 0] = mc
    cst[0, 1] = l0 * g0 + pst[1] * g1
    for p in CHIP_FAR:
        send(cst.at[0], cst.at[cid(p)], cst_s.at[cid(p)], cst_r.at[cid(p)], chip_dev(p))
    scale0 = jnp.broadcast_to(g0[0:1, :], (128, 128)).T
    scale1 = jnp.broadcast_to(g1[0:1, :], (128, 128)).T

    def unit(ref, k):
        near = ref[pl.ds(8 * x_hi + k, NZ, stride=16), :]
        far = ref[pl.ds(8 * (1 - x_hi) + k + 1 - 2 * lax.rem(k, 2), NZ, stride=16), :]
        return jnp.concatenate([near, far], axis=0)

    for n, w in ((0, 2), (2, 2), (4, 1)):
        arrived(precv.at[pl.ds(n, w)], pp_s.at[n], pp_r.at[n])
        for q in range(n, n + w):
            pown[q] = pown[q] * scale0 + precv[q] * scale1
    older = len(live)
    for p in CHIP_FAR:
        for n in range(5):
            rs_send[cid(p), :, pl.ds(n * 128, 128)] = unit(pown.at[n], chip_at(p)).astype(BF)
        send(rs_send.at[cid(p)], rs_recv.at[cid(p)], rs_s.at[cid(p)], rs_r.at[cid(p)], chip_dev(p))
    yown = jnp.concatenate([unit(pown.at[n], chip) for n in range(5)], axis=1)

    for n in range(4):
        part = pl.ds(n * 256, 256)
        v = lg[:, part]
        ex = jnp.exp(v - jnp.max(v, axis=0, keepdims=True))
        ex = ex / jnp.sum(ex, axis=0, keepdims=True)
        mxs[2 * n] = ex[:, :128]
        mxs[2 * n + 1] = ex[:, 128:]
    for n in range(8):
        part = pl.ds(n * 128, 128)
        rows = []
        for k in range(K):
            rows.append(mxs[n, pl.ds(8 * x_hi + k, NZ, stride=16), :])
            rows.append(mxs[n, pl.ds(8 * (1 - x_hi) + k, NZ, stride=16), :])
        mw[part, :] = jnp.concatenate(rows, axis=0).T.astype(BF)

    drain(older)

    for p in CHIP_NEAR:
        arrived(cst.at[cid(p)], cst_s.at[cid(p)], cst_r.at[cid(p)])
    top = cst[0, 0]
    for j in range(1, NC):
        top = jnp.maximum(top, cst[j, 0])
    total = jnp.zeros((8, 128), F32)
    for j in range(NC):
        total += cst[j, 1] * jnp.exp(cst[j, 0] - top)
    row = lax.broadcasted_iota(jnp.int32, (8, 128), 0)
    factors = jnp.zeros((8, 128), F32)
    for j in range(NC):
        factors = jnp.where(row == j, jnp.exp(cst[j, 0] - top) / total, factors)
    fin[0:8, :] = factors
    ft[...] = fin[...].T
    fk = unit(ft, chip)

    acc = yown * fk[:, 0:1]
    for p in CHIP_NEAR:
        j = cid(p)
        arrived(rs_recv.at[j], rs_s.at[j], rs_r.at[j])
        acc += rs_recv[j].astype(F32) * fk[:, j : j + 1]

    def rows_across(value, rows, recv, ssem, rsem):
        older = len(live)
        rows[...] = value.reshape(NE, 1, HALF)
        for i in EXP_FAR:
            src = rows.at[i[0] * NZ + lax.rem(z + i[1], NZ)]
            send(src, recv.at[i[0] * NZ + z], ssem.at[eid(i)], rsem.at[eid(i)], exp_dev(i))
        recv[z] = rows[z]
        drain(older)
        for i in EXP_NEAR:
            dst = recv.at[i[0] * NZ + lax.rem(z + NZ - i[1], NZ)]
            arrived(dst, ssem.at[eid(i)], rsem.at[eid(i)])
        return recv[...].reshape(NE, HALF)

    def spread(value, buf, gs, gr):
        older = len(live)
        buf[h, chip] = value
        for p in CHIP_FAR:
            send(buf.at[h, chip], buf.at[h, chip], gs.at[cid(p)], gr.at[cid(p)], chip_dev(p))
        drain(older)

    def forward(q, buf, gs, gr, fs, fr):
        for p in ((q, 1), (q, 0)) if q else ((q, 1),):
            arrived(buf.at[h, chip_from(p)], gs.at[cid(p)], gr.at[cid(p)])
        src = buf.at[h, pl.ds(lax.rem(y + 4 - q, 4) * 2, 2)]
        send(src, src, fs.at[q], fr.at[q], sib)

    def other_half(q, buf, fs, fr):
        arrived(buf.at[o, pl.ds(lax.rem(y + 4 - q, 4) * 2, 2)], fs.at[q], fr.at[q])

    across = rows_across(acc, a_send, a_recv, a_s, a_r)
    spread(across.astype(BF), xb, xg_s, xg_r)
    for c in loads[4:]:
        c.wait()

    def experts(q):
        ks = (chip_from((q, 0)), chip_from((q, 1)))
        other_half(q, xb, xf_s, xf_r)
        inner = [nt(xb[0, k], upv[0, k]) + nt(xb[1, k], upv[1, k]) for k in ks]
        hidden = [gelu(v).astype(BF) for v in inner]
        away = [mm(v, dnv[o, k]) for v, k in zip(hidden, ks)]
        for n in range(2):
            po_send[q, n] = away[n]
        send(po_send.at[q], po_recv.at[q], po_s.at[q], po_r.at[q], sib)
        here = [mm(v, dnv[h, k]) for v, k in zip(hidden, ks)]
        for n in range(2):
            po_own[q, n] = here[n]

    def reduce_on(q):
        arrived(po_recv.at[q], po_s.at[q], po_r.at[q])
        both = [po_own[q, n] + po_recv[q, n] for n in range(2)]
        for n in range(2):
            value = jnp.concatenate([both[n][:NZ], both[1 - n][NZ:]], axis=0)
            if q or n:
                ro_send[q, n] = value.astype(BF)
                p = (4 - q if q else 0, n)
                sems = ro_s.at[cid(p)], ro_r.at[cid(p)]
                send(ro_send.at[q, n], ro_recv.at[cid(p)], *sems, chip_dev(p))
            else:
                po_own[0, 0] = value

    forward(0, xb, xg_s, xg_r, xf_s, xf_r)
    forward(1, xb, xg_s, xg_r, xf_s, xf_r)
    forward(3, xb, xg_s, xg_r, xf_s, xf_r)
    experts(0)
    experts(1)
    forward(2, xb, xg_s, xg_r, xf_s, xf_r)
    reduce_on(0)
    experts(3)
    reduce_on(1)
    experts(2)
    older = len(live)
    reduce_on(3)
    reduce_on(2)
    acc = po_own[0, 0]
    drain(older)
    for p in CHIP_NEAR:
        arrived(ro_recv.at[cid(p)], ro_s.at[cid(p)], ro_r.at[cid(p)])
        acc += ro_recv[cid(p)].astype(F32)

    across = rows_across(acc, b_send, b_recv, b_s, b_r)
    spread(across.astype(BF), ret, rg_s, rg_r)
    for q in (0, 1, 3, 2):
        forward(q, ret, rg_s, rg_r, rf_s, rf_r)

    def mix(half):
        table = ret[half].reshape(SLOTS, HALF)
        lanes = pl.ds(pl.multiple_of(half * HALF, 128), HALF)
        for n in range(4):
            part = pl.ds(n * 256, 256)
            out_ref[part, lanes] = mm(mw[part, :], table).astype(BF)

    mix(h)
    for q in (0, 1, 3, 2):
        other_half(q, ret, rf_s, rf_r)
    mix(o)
    drain()


def shards(tokens, slot_params, up_weight, down_weight):
    vm = pltpu.VMEM
    dma = pltpu.SemaphoreType.DMA
    call = pl.pallas_call(
        kernel,
        out_shape=jax.ShapeDtypeStruct((ROWS, 2 * HALF), BF),
        in_specs=[pl.BlockSpec(memory_space=pltpu.HBM)] * 4,
        out_specs=pl.BlockSpec(memory_space=pltpu.VMEM),
        scratch_shapes=[
            vm((2, ROWS, HALF), BF),
            vm((2, K, FD, HALF), BF),
            vm((2, K, FD, HALF), BF),
            vm((2, NE, K, HALF), BF),
            vm((SLOTS, ROWS), F32),
            vm((SLOTS, ROWS), BF),
            vm((SLOTS, 128), F32),
            vm((2, 8, 128), F32),
            vm((2, 8, 128), F32),
            vm((NC, 2, 8, 128), F32),
            vm((128, 128), F32),
            vm((128, 128), F32),
            vm((5, SLOTS, 128), F32),
            vm((5, SLOTS, 128), F32),
            vm((5, SLOTS, 128), F32),
            vm((NC, NE, HALF), BF),
            vm((NC, NE, HALF), BF),
            vm((NE, 1, HALF), F32),
            vm((NE, 1, HALF), F32),
            vm((2, NC, NE, HALF), BF),
            vm((4, 2, NE, HALF), F32),
            vm((4, 2, NE, HALF), F32),
            vm((4, 2, NE, HALF), F32),
            vm((4, 2, NE, HALF), BF),
            vm((NC, NE, HALF), BF),
            vm((NE, 1, HALF), F32),
            vm((NE, 1, HALF), F32),
            vm((2, NC, NE, HALF), BF),
            vm((8, SLOTS, 128), F32),
            vm((ROWS, SLOTS), BF),
            dma((8,)),
            dma((NE,)), dma((NE,)), dma((NE,)), dma((NE,)),
            dma, dma,
            dma((NC,)), dma((NC,)),
            dma((5,)), dma((5,)),
            dma((NC,)), dma((NC,)),
            dma((NE,)), dma((NE,)),
            dma((NC,)), dma((NC,)), dma((4,)), dma((4,)),
            dma((4,)), dma((4,)),
            dma((NC,)), dma((NC,)),
            dma((NE,)), dma((NE,)),
            dma((NC,)), dma((NC,)), dma((4,)), dma((4,)),
        ],
        compiler_params=pltpu.CompilerParams(
            collective_id=0, has_side_effects=True, vmem_limit_bytes=50 * 2**20
        ),
        cost_estimate=pl.CostEstimate(flops=1_400_000_000, bytes_accessed=14_000_000, transcendentals=400_000),
        name="soft_moe",
    )
    mixed = call(
        tokens.reshape(ROWS, 2 * HALF),
        slot_params.T,
        jnp.transpose(up_weight, (0, 2, 1)),
        down_weight,
    )
    return mixed.reshape(tokens.shape)


def solution(mesh):
    in_specs = (
        P("expert", "seq", None),
        P(None, "expert"),
        P("expert", None, "seq"),
        P("expert", "seq", None),
    )
    out_specs = P("expert", "seq", None)
    return jax.shard_map(shards, mesh=mesh, in_specs=in_specs, out_specs=out_specs, check_vma=False)
```

```python
import jax
import jax.numpy as jnp
from jax import lax
from jax.experimental import pallas as pl
from jax.experimental.pallas import tpu as pltpu
from jax.sharding import PartitionSpec as P

MESH = pl.DeviceIdType.MESH
BF = jnp.bfloat16
F32 = jnp.float32
NE = 16
NZ = 8
NC = 8
K = 8
HALF = 640
ROWS = 1024
FD = 160
SLOTS = NE * K

EXP_FAR = (
    (1, 4), (1, 3), (1, 5), (0, 4), (1, 2), (1, 6), (0, 3), (0, 5),
    (1, 1), (1, 7), (0, 2), (0, 6), (1, 0), (0, 1), (0, 7),
)
EXP_NEAR = tuple(reversed(EXP_FAR))
CHIP_FAR = ((2, 1), (2, 0), (1, 1), (3, 1), (1, 0), (3, 0), (0, 1))
CHIP_NEAR = tuple(reversed(CHIP_FAR))


def nt(a, b):
    return lax.dot_general(a, b, (((1,), (1,)), ((), ())), preferred_element_type=F32)


def mm(a, b):
    return jnp.dot(a, b, preferred_element_type=F32)


def gelu(v):
    return 0.5 * v * (1.0 + lax.erf(v * 0.7071067811865476))


def kernel(
    tok_hbm, sp_hbm, up_hbm, dn_hbm, out_ref,
    tokh, upv, dnv, tab, lg, wt, xs, stat, pst, cst, fin, ft,
    psend, pown, precv, rs_send, rs_recv, a_send, a_recv, xb,
    px_send, px_recv, ro_send, ro_own, ro_recv, b_send, b_recv, ret, mxs, mw,
    load_sem, tab_s, tab_r, tabf_s, tabf_r, pst_s, pst_r, cst_s, cst_r, pp_s, pp_r,
    rs_s, rs_r, w_s, w_r, a_s, a_r, xg_s, xg_r, px_s, px_r, ro_s, ro_r, b_s, b_r,
    rg_s, rg_r, rf_s, rf_r,
):
    s = lax.axis_index("seq")
    e = lax.axis_index("expert")
    chip = lax.div(s, 2)
    h = lax.rem(s, 2)
    o = 1 - h
    y = lax.div(chip, 2)
    x_lo = lax.rem(chip, 2)
    z = lax.div(e, 2)
    x_hi = lax.rem(e, 2)
    sib = (chip * 2 + o, e)
    flipped = y * 2 + 1 - x_lo

    def chip_at(p):
        return lax.rem(y + p[0], 4) * 2 + (1 - x_lo if p[1] else x_lo)

    def chip_from(p):
        return chip_at((4 - p[0], p[1]))

    def chip_dev(p):
        return (chip_at(p) * 2 + h, e)

    def exp_at(i):
        return lax.rem(z + i[1], NZ) * 2 + (1 - x_hi if i[0] else x_hi)

    def exp_from(i):
        return exp_at((i[0], NZ - i[1]))

    def exp_dev(i):
        return ((flipped if i[0] else chip) * 2 + h, exp_at(i))

    def cid(p):
        return p[0] * 2 + p[1]

    def eid(i):
        return i[0] * NZ + i[1]

    live = []

    def drain(groups=None):
        for item in list(live):
            if groups is None or item[0] in groups:
                item[1].wait_send()
                live.remove(item)

    def copy(src, dst, ssem, rsem, dev):
        return pltpu.make_async_remote_copy(
            src_ref=src, dst_ref=dst, send_sem=ssem, recv_sem=rsem, device_id=dev, device_id_type=MESH
        )

    def send(group, src, dst, ssem, rsem, dev):
        c = copy(src, dst, ssem, rsem, dev)
        c.start()
        live.append((group, c))

    def arrived(dst, ssem, rsem):
        copy(dst, dst, ssem, rsem, sib).wait_recv()

    barrier = pltpu.get_barrier_semaphore()
    for i in EXP_FAR:
        pl.semaphore_signal(barrier, inc=1, device_id=exp_dev(i), device_id_type=MESH)
    for p in CHIP_FAR:
        pl.semaphore_signal(barrier, inc=1, device_id=chip_dev(p), device_id_type=MESH)
    for p in CHIP_FAR:
        pl.semaphore_signal(barrier, inc=1, device_id=(chip_at(p) * 2 + o, e), device_id_type=MESH)
    pl.semaphore_signal(barrier, inc=1, device_id=sib, device_id_type=MESH)

    loads = []
    for half in range(2):
        lanes = pl.ds(half * HALF, HALF)
        c = pltpu.make_async_copy(sp_hbm.at[:, lanes], tab.at[half, e], load_sem.at[4 + half])
        c.start()
        loads.append(c)
    for half in range(2):
        c = pltpu.make_async_copy(tok_hbm.at[:, pl.ds(half * HALF, HALF)], tokh.at[half], load_sem.at[half])
        c.start()
        loads.append(c)
    ours = pl.ds(pl.multiple_of(h * HALF, 128), HALF)
    units = pl.ds(pl.multiple_of(h * FD, 16), FD)
    their_units = pl.ds(pl.multiple_of(o * FD, 16), FD)
    for n, (src, dst) in enumerate(((up_hbm, upv), (dn_hbm, dnv))):
        c = pltpu.make_async_copy(src.at[:, :, ours], dst.at[:, units], load_sem.at[2 + n])
        c.start()
        loads.append(c)
    fin[...] = jnp.zeros_like(fin)
    px_send[...] = jnp.zeros_like(px_send)
    loads[0].wait()
    loads[1].wait()
    pl.semaphore_wait(barrier, NE - 1 + 2 * (NC - 1) + 1)

    for i in EXP_FAR:
        send("tab", tab.at[h, e], tab.at[h, e], tab_s.at[eid(i)], tab_r.at[eid(i)], exp_dev(i))
    for i in EXP_NEAR:
        src = tab.at[h, exp_from(i)]
        arrived(src, tab_s.at[eid(i)], tab_r.at[eid(i)])
        send("tab", src, src, tabf_s.at[eid(i)], tabf_r.at[eid(i)], sib)
    loads[2].wait()
    loads[3].wait()
    half_table = tab[h].astype(F32).reshape(SLOTS, HALF).astype(BF)
    for n in range(4):
        part = pl.ds(n * 256, 256)
        lg[:, part] = nt(half_table, tokh[h, part, :])
    for i in EXP_NEAR:
        arrived(tab.at[o, exp_from(i)], tabf_s.at[eid(i)], tabf_r.at[eid(i)])
    half_table = tab[o].astype(F32).reshape(SLOTS, HALF).astype(BF)
    for n in range(4):
        part = pl.ds(n * 256, 256)
        lg[:, part] += nt(half_table, tokh[o, part, :])

    lane = lax.broadcasted_iota(jnp.int32, (32, 128), 1)
    for r in range(0, SLOTS, 32):
        part = pl.ds(r, 32)
        v = lg[part, :]
        m = jnp.max(v, axis=1, keepdims=True)
        ex = jnp.exp(v - m)
        l = jnp.sum(ex, axis=1, keepdims=True)
        wt[part, :] = ex.astype(BF)
        xs[part, :] = jnp.where(lane < 64, m, l)
    xt = xs[...].T
    m0 = jnp.broadcast_to(xt[0:1, :], (8, 128))
    l0 = jnp.broadcast_to(xt[64:65, :], (8, 128))
    stat[0] = m0
    stat[1] = l0
    send("tab", stat, pst, pst_s, pst_r, sib)

    for n, w in ((0, 2), (2, 2), (4, 1)):
        sums = mm(wt[...], tokh[o, :, pl.ds(n * 128, w * 128)])
        for q in range(w):
            psend[n + q] = sums[:, q * 128 : q * 128 + 128]
        part = pl.ds(n, w)
        send("pp", psend.at[part], precv.at[part], pp_s.at[n], pp_r.at[n], sib)
    sums = mm(wt[...], tokh[h])
    for n in range(5):
        pown[n] = sums[:, n * 128 : n * 128 + 128]
    arrived(pst, pst_s, pst_r)
    m1 = pst[0]
    mc = jnp.maximum(m0, m1)
    g0 = jnp.exp(m0 - mc)
    g1 = jnp.exp(m1 - mc)
    cst[0, 0] = mc
    cst[0, 1] = l0 * g0 + pst[1] * g1
    for p in CHIP_FAR:
        send("pp", cst.at[0], cst.at[cid(p)], cst_s.at[cid(p)], cst_r.at[cid(p)], chip_dev(p))
    scale0 = jnp.broadcast_to(g0[0:1, :], (128, 128)).T
    scale1 = jnp.broadcast_to(g1[0:1, :], (128, 128)).T

    def unit(ref, k):
        near = ref[pl.ds(8 * x_hi + k, NZ, stride=16), :]
        far = ref[pl.ds(8 * (1 - x_hi) + k + 1 - 2 * lax.rem(k, 2), NZ, stride=16), :]
        return jnp.concatenate([near, far], axis=0)

    for n, w in ((0, 2), (2, 2), (4, 1)):
        arrived(precv.at[pl.ds(n, w)], pp_s.at[n], pp_r.at[n])
        for q in range(n, n + w):
            pown[q] = pown[q] * scale0 + precv[q] * scale1
    for p in CHIP_FAR:
        for n in range(5):
            rs_send[cid(p), :, pl.ds(n * 128, 128)] = unit(pown.at[n], chip_at(p)).astype(BF)
        send("rs", rs_send.at[cid(p)], rs_recv.at[cid(p)], rs_s.at[cid(p)], rs_r.at[cid(p)], chip_dev(p))
    theirs = pl.ds(pl.multiple_of(o * HALF, 128), HALF)
    send("w", up_hbm.at[:, :, theirs], upv.at[:, units], w_s.at[0], w_r.at[0], sib)
    send("w", dn_hbm.at[:, :, theirs], dnv.at[:, units], w_s.at[1], w_r.at[1], sib)
    yown = jnp.concatenate([unit(pown.at[n], chip) for n in range(5)], axis=1)

    for n in range(4):
        part = pl.ds(n * 256, 256)
        v = lg[:, part]
        ex = jnp.exp(v - jnp.max(v, axis=0, keepdims=True))
        ex = ex / jnp.sum(ex, axis=0, keepdims=True)
        mxs[2 * n] = ex[:, :128]
        mxs[2 * n + 1] = ex[:, 128:]
    for n in range(8):
        part = pl.ds(n * 128, 128)
        rows = []
        for k in range(K):
            rows.append(mxs[n, pl.ds(8 * x_hi + k, NZ, stride=16), :])
            rows.append(mxs[n, pl.ds(8 * (1 - x_hi) + k, NZ, stride=16), :])
        mw[part, :] = jnp.concatenate(rows, axis=0).T.astype(BF)

    drain(("tab",))

    for p in CHIP_NEAR:
        arrived(cst.at[cid(p)], cst_s.at[cid(p)], cst_r.at[cid(p)])
    top = cst[0, 0]
    for j in range(1, NC):
        top = jnp.maximum(top, cst[j, 0])
    total = jnp.zeros((8, 128), F32)
    for j in range(NC):
        total += cst[j, 1] * jnp.exp(cst[j, 0] - top)
    row = lax.broadcasted_iota(jnp.int32, (8, 128), 0)
    factors = jnp.zeros((8, 128), F32)
    for j in range(NC):
        factors = jnp.where(row == j, jnp.exp(cst[j, 0] - top) / total, factors)
    fin[0:8, :] = factors
    ft[...] = fin[...].T
    fk = unit(ft, chip)

    acc = yown * fk[:, 0:1]
    for p in CHIP_NEAR:
        j = cid(p)
        arrived(rs_recv.at[j], rs_s.at[j], rs_r.at[j])
        acc += rs_recv[j].astype(F32) * fk[:, j : j + 1]

    def rows_across(group, value, rows, recv, ssem, rsem, idle):
        rows[...] = value.reshape(NE, 1, HALF)
        for i in EXP_FAR:
            src = rows.at[i[0] * NZ + lax.rem(z + i[1], NZ)]
            send(group, src, recv.at[i[0] * NZ + z], ssem.at[eid(i)], rsem.at[eid(i)], exp_dev(i))
        recv[z] = rows[z]
        drain(idle)
        for i in EXP_NEAR:
            dst = recv.at[i[0] * NZ + lax.rem(z + NZ - i[1], NZ)]
            arrived(dst, ssem.at[eid(i)], rsem.at[eid(i)])
        return recv[...].reshape(NE, HALF)

    across = rows_across("a", acc, a_send, a_recv, a_s, a_r, ("pp",))
    xb[chip] = across.astype(BF)
    for p in CHIP_FAR:
        send("xg", xb.at[chip], xb.at[chip], xg_s.at[cid(p)], xg_r.at[cid(p)], chip_dev(p))
    for c in loads[4:]:
        c.wait()
    arrived(upv.at[:, their_units], w_s.at[0], w_r.at[0])
    arrived(dnv.at[:, their_units], w_s.at[1], w_r.at[1])

    def first(q):
        for p in ((q, 1), (q, 0)) if q else ((q, 1),):
            arrived(xb.at[chip_from(p)], xg_s.at[cid(p)], xg_r.at[cid(p)])
        for n in range(2):
            k = chip_from((q, n))
            px_send[q, n, :, pl.ds(0, 2 * FD)] = nt(xb[k], upv[k])
        send("px", px_send.at[q], px_recv.at[q], px_s.at[q], px_r.at[q], sib)

    def second(q):
        arrived(px_recv.at[q], px_s.at[q], px_r.at[q])
        both = []
        for n in range(2):
            k = chip_from((q, n))
            inner = px_send[q, n, :, pl.ds(0, 2 * FD)] + px_recv[q, n, :, pl.ds(0, 2 * FD)]
            both.append(mm(gelu(inner).astype(BF), dnv[k]))
        for n in range(2):
            value = jnp.concatenate([both[n][:NZ], both[1 - n][NZ:]], axis=0)
            if q or n:
                ro_send[q, n] = value.astype(BF)
                p = (4 - q if q else 0, n)
                sems = ro_s.at[cid(p)], ro_r.at[cid(p)]
                send("ro", ro_send.at[q, n], ro_recv.at[cid(p)], *sems, chip_dev(p))
            else:
                ro_own[...] = value

    first(0)
    first(1)
    first(3)
    second(0)
    first(2)
    second(1)
    second(3)
    second(2)
    acc = ro_own[...]
    drain(("rs", "a", "xg"))
    for p in CHIP_NEAR:
        arrived(ro_recv.at[cid(p)], ro_s.at[cid(p)], ro_r.at[cid(p)])
        acc += ro_recv[cid(p)].astype(F32)

    across = rows_across("b", acc, b_send, b_recv, b_s, b_r, ("px", "w"))
    ret[h, chip] = across.astype(BF)
    for p in CHIP_FAR:
        send("rg", ret.at[h, chip], ret.at[h, chip], rg_s.at[cid(p)], rg_r.at[cid(p)], chip_dev(p))
        send("rg", ret.at[h, chip], ret.at[h, chip], rf_s.at[cid(p)], rf_r.at[cid(p)], (chip_at(p) * 2 + o, e))
    send("rg", ret.at[h, chip], ret.at[h, chip], rf_s.at[0], rf_r.at[0], sib)
    drain(("ro", "b"))
    for p in CHIP_NEAR:
        arrived(ret.at[h, chip_from(p)], rg_s.at[cid(p)], rg_r.at[cid(p)])

    def mix(half):
        table = ret[half].reshape(SLOTS, HALF)
        lanes = pl.ds(pl.multiple_of(half * HALF, 128), HALF)
        for n in range(4):
            part = pl.ds(n * 256, 256)
            out_ref[part, lanes] = mm(mw[part, :], table).astype(BF)

    mix(h)
    for p in ((0, 0),) + CHIP_NEAR:
        arrived(ret.at[o, chip_from(p)], rf_s.at[cid(p)], rf_r.at[cid(p)])
    mix(o)
    drain()


def shards(tokens, slot_params, up_weight, down_weight):
    vm = pltpu.VMEM
    dma = pltpu.SemaphoreType.DMA
    call = pl.pallas_call(
        kernel,
        out_shape=jax.ShapeDtypeStruct((ROWS, 2 * HALF), BF),
        in_specs=[pl.BlockSpec(memory_space=pltpu.HBM)] * 4,
        out_specs=pl.BlockSpec(memory_space=pltpu.VMEM),
        scratch_shapes=[
            vm((2, ROWS, HALF), BF),
            vm((K, 2 * FD, HALF), BF),
            vm((K, 2 * FD, HALF), BF),
            vm((2, NE, K, HALF), BF),
            vm((SLOTS, ROWS), F32),
            vm((SLOTS, ROWS), BF),
            vm((SLOTS, 128), F32),
            vm((2, 8, 128), F32),
            vm((2, 8, 128), F32),
            vm((NC, 2, 8, 128), F32),
            vm((128, 128), F32),
            vm((128, 128), F32),
            vm((5, SLOTS, 128), F32),
            vm((5, SLOTS, 128), F32),
            vm((5, SLOTS, 128), F32),
            vm((NC, NE, HALF), BF),
            vm((NC, NE, HALF), BF),
            vm((NE, 1, HALF), F32),
            vm((NE, 1, HALF), F32),
            vm((NC, NE, HALF), BF),
            vm((4, 2, NE, 384), F32),
            vm((4, 2, NE, 384), F32),
            vm((4, 2, NE, HALF), BF),
            vm((NE, HALF), F32),
            vm((NC, NE, HALF), BF),
            vm((NE, 1, HALF), F32),
            vm((NE, 1, HALF), F32),
            vm((2, NC, NE, HALF), BF),
            vm((8, SLOTS, 128), F32),
            vm((ROWS, SLOTS), BF),
            dma((8,)),
            dma((NE,)), dma((NE,)), dma((NE,)), dma((NE,)),
            dma, dma,
            dma((NC,)), dma((NC,)),
            dma((5,)), dma((5,)),
            dma((NC,)), dma((NC,)),
            dma((2,)), dma((2,)),
            dma((NE,)), dma((NE,)),
            dma((NC,)), dma((NC,)),
            dma((4,)), dma((4,)),
            dma((NC,)), dma((NC,)),
            dma((NE,)), dma((NE,)),
            dma((NC,)), dma((NC,)), dma((NC,)), dma((NC,)),
        ],
        compiler_params=pltpu.CompilerParams(
            collective_id=0, has_side_effects=True, vmem_limit_bytes=50 * 2**20
        ),
        cost_estimate=pl.CostEstimate(flops=1_400_000_000, bytes_accessed=14_000_000, transcendentals=400_000),
        name="soft_moe",
    )
    operands = (tokens.reshape(ROWS, 2 * HALF), slot_params.T, jnp.transpose(up_weight, (0, 2, 1)), down_weight)
    mixed = call(*(pltpu.with_memory_space_constraint(v, pltpu.HBM) for v in operands))
    return mixed.reshape(tokens.shape)


def solution(mesh):
    in_specs = (
        P("expert", "seq", None),
        P(None, "expert"),
        P("expert", None, "seq"),
        P("expert", "seq", None),
    )
    out_specs = P("expert", "seq", None)
    return jax.shard_map(shards, mesh=mesh, in_specs=in_specs, out_specs=out_specs, check_vma=False)
```

```python
import functools

import jax
import jax.numpy as jnp
from jax import lax
from jax.experimental import pallas as pl
from jax.experimental.pallas import tpu as pltpu
from jax.sharding import PartitionSpec as P

MESH = pl.DeviceIdType.MESH
BF = jnp.bfloat16
F32 = jnp.float32
NE = 16
NZ = 8
NC = 8
K = 8
HALF = 640
ROWS = 1024
FD = 160
SLOTS = NE * K
PADDED = SLOTS + 16

EXP_FAR = (
    (1, 4), (1, 3), (1, 5), (0, 4), (1, 2), (1, 6), (0, 3), (0, 5),
    (1, 1), (1, 7), (0, 2), (0, 6), (1, 0), (0, 1), (0, 7),
)
EXP_NEAR = tuple(reversed(EXP_FAR))
CHIP_FAR = ((2, 1), (2, 0), (1, 1), (3, 1), (1, 0), (3, 0), (0, 1))
CHIP_NEAR = tuple(reversed(CHIP_FAR))


def nt(a, b):
    return lax.dot_general(a, b, (((1,), (1,)), ((), ())), preferred_element_type=F32)


def mm(a, b):
    return jnp.dot(a, b, preferred_element_type=F32)


def gelu(v):
    return 0.5 * v * (1.0 + lax.erf(v * 0.7071067811865476))


def kernel(
    tok_hbm, sp_hbm, up_hbm, dn_hbm, out_ref,
    tokh, upv, dnv, tab, lg, wt, xs, stat, pst, cst, fin, ft,
    psend, pown, precv, rs_send, rs_recv, a_send, a_recv, xb,
    px_send, px_recv, ro_send, ro_own, ro_recv, b_send, b_recv, ret, mxs, mw,
    load_sem, tab_s, tab_r, tabf_s, tabf_r, pst_s, pst_r, cst_s, cst_r, pp_s, pp_r,
    rs_s, rs_r, w_s, w_r, a_s, a_r, xg_s, xg_r, px_s, px_r, ro_s, ro_r, b_s, b_r,
    rg_s, rg_r,
):
    s = lax.axis_index("seq")
    e = lax.axis_index("expert")
    chip = lax.div(s, 2)
    h = lax.rem(s, 2)
    o = 1 - h
    y = lax.div(chip, 2)
    x_lo = lax.rem(chip, 2)
    z = lax.div(e, 2)
    x_hi = lax.rem(e, 2)
    sib = (chip * 2 + o, e)
    flipped = y * 2 + 1 - x_lo

    def chip_at(p):
        return lax.rem(y + p[0], 4) * 2 + (1 - x_lo if p[1] else x_lo)

    def chip_from(p):
        return chip_at((4 - p[0], p[1]))

    def chip_dev(p):
        return (chip_at(p) * 2 + h, e)

    def exp_at(i):
        return lax.rem(z + i[1], NZ) * 2 + (1 - x_hi if i[0] else x_hi)

    def exp_dev(i):
        return ((flipped if i[0] else chip) * 2 + h, exp_at(i))

    def cid(p):
        return p[0] * 2 + p[1]

    def eid(i):
        return i[0] * NZ + i[1]

    def place_to(i):
        return i[0] * NZ + (i[1] + 1) % NZ

    def place_from(i):
        return i[0] * NZ + (1 - i[1]) % NZ

    live = []

    def drain(groups=None):
        for item in list(live):
            if groups is None or item[0] in groups:
                item[1].wait_send()
                live.remove(item)

    def copy(src, dst, ssem, rsem, dev):
        return pltpu.make_async_remote_copy(
            src_ref=src, dst_ref=dst, send_sem=ssem, recv_sem=rsem, device_id=dev, device_id_type=MESH
        )

    def send(group, src, dst, ssem, rsem, dev):
        c = copy(src, dst, ssem, rsem, dev)
        c.start()
        live.append((group, c))

    def arrived(dst, ssem, rsem):
        copy(dst, dst, ssem, rsem, sib).wait_recv()

    barrier = pltpu.get_barrier_semaphore()
    for i in EXP_FAR:
        pl.semaphore_signal(barrier, inc=1, device_id=exp_dev(i), device_id_type=MESH)
    for p in CHIP_FAR:
        pl.semaphore_signal(barrier, inc=1, device_id=chip_dev(p), device_id_type=MESH)
    for p in CHIP_FAR:
        pl.semaphore_signal(barrier, inc=1, device_id=(chip_at(p) * 2 + o, e), device_id_type=MESH)
    pl.semaphore_signal(barrier, inc=1, device_id=sib, device_id_type=MESH)

    loads = []
    for half in range(2):
        lanes = pl.ds(half * HALF, HALF)
        c = pltpu.make_async_copy(sp_hbm.at[:, lanes], tab.at[half, 1], load_sem.at[4 + half])
        c.start()
        loads.append(c)
    for half in range(2):
        c = pltpu.make_async_copy(tok_hbm.at[:, pl.ds(half * HALF, HALF)], tokh.at[half], load_sem.at[half])
        c.start()
        loads.append(c)
    ours = pl.ds(pl.multiple_of(h * HALF, 128), HALF)
    units = pl.ds(pl.multiple_of(h * FD, 16), FD)
    their_units = pl.ds(pl.multiple_of(o * FD, 16), FD)
    for n, (src, dst) in enumerate(((up_hbm, upv), (dn_hbm, dnv))):
        c = pltpu.make_async_copy(src.at[:, :, ours], dst.at[:, units], load_sem.at[2 + n])
        c.start()
        loads.append(c)
    fin[...] = jnp.zeros_like(fin)
    px_send[...] = jnp.zeros_like(px_send)
    loads[0].wait()
    loads[1].wait()
    pl.semaphore_wait(barrier, NE - 1 + 2 * (NC - 1) + 1)

    for i in EXP_FAR:
        send("tab", tab.at[h, 1], tab.at[h, place_from(i)], tab_s.at[eid(i)], tab_r.at[eid(i)], exp_dev(i))
    for i in EXP_NEAR:
        src = tab.at[h, place_from(i)]
        arrived(src, tab_s.at[eid(i)], tab_r.at[eid(i)])
        send("tab", src, src, tabf_s.at[eid(i)], tabf_r.at[eid(i)], sib)
    loads[2].wait()
    loads[3].wait()
    half_table = tab[h].astype(F32).reshape(SLOTS, HALF).astype(BF)
    for n in range(4):
        part = pl.ds(n * 256, 256)
        lg[:, part] = nt(half_table, tokh[h, part, :])
    for i in EXP_NEAR:
        arrived(tab.at[o, place_from(i)], tabf_s.at[eid(i)], tabf_r.at[eid(i)])
    half_table = tab[o].astype(F32).reshape(SLOTS, HALF).astype(BF)
    for n in range(4):
        part = pl.ds(n * 256, 256)
        lg[:, part] += nt(half_table, tokh[o, part, :])

    lane = lax.broadcasted_iota(jnp.int32, (32, 128), 1)
    for r in range(0, SLOTS, 32):
        part = pl.ds(r, 32)
        v = lg[part, :]
        m = jnp.max(v, axis=1, keepdims=True)
        ex = jnp.exp(v - m)
        l = jnp.sum(ex, axis=1, keepdims=True)
        wt[part, :] = ex.astype(BF)
        xs[part, :] = jnp.where(lane < 64, m, l)
    xt = xs[...].T
    m0 = jnp.broadcast_to(xt[0:1, :], (8, 128))
    l0 = jnp.broadcast_to(xt[64:65, :], (8, 128))
    stat[0] = m0
    stat[1] = l0
    send("tab", stat, pst, pst_s, pst_r, sib)

    for n, w in ((0, 2), (2, 2), (4, 1)):
        sums = mm(wt[...], tokh[o, :, pl.ds(n * 128, w * 128)])
        for q in range(w):
            psend[n + q] = sums[:, q * 128 : q * 128 + 128]
        part = pl.ds(n, w)
        send("pp", psend.at[part], precv.at[part], pp_s.at[n], pp_r.at[n], sib)
    sums = mm(wt[...], tokh[h])
    all_rows = pl.ds(0, SLOTS)
    for n in range(5):
        pown[n, all_rows, :] = sums[:, n * 128 : n * 128 + 128]
    arrived(pst, pst_s, pst_r)
    m1 = pst[0]
    mc = jnp.maximum(m0, m1)
    g0 = jnp.exp(m0 - mc)
    g1 = jnp.exp(m1 - mc)
    cst[0, 0] = mc
    cst[0, 1] = l0 * g0 + pst[1] * g1
    for p in CHIP_FAR:
        send("pp", cst.at[0], cst.at[cid(p)], cst_s.at[cid(p)], cst_r.at[cid(p)], chip_dev(p))
    scale0 = jnp.broadcast_to(g0[0:1, :], (128, 128)).T
    scale1 = jnp.broadcast_to(g1[0:1, :], (128, 128)).T

    def unit(ref, k):
        near = ref[pl.ds(k, NZ, stride=K), :]
        far = ref[pl.ds(NZ * K + k + 1 - 2 * lax.rem(k, 2), NZ, stride=K), :]
        return jnp.concatenate([near, far], axis=0)

    for n, w in ((0, 2), (2, 2), (4, 1)):
        arrived(precv.at[pl.ds(n, w)], pp_s.at[n], pp_r.at[n])
        for q in range(n, n + w):
            pown[q, all_rows, :] = pown[q, all_rows, :] * scale0 + precv[q] * scale1
    for p in CHIP_FAR:
        for n in range(5):
            rs_send[cid(p), :, pl.ds(n * 128, 128)] = unit(pown.at[n], chip_at(p)).astype(BF)
        send("rs", rs_send.at[cid(p)], rs_recv.at[cid(p)], rs_s.at[cid(p)], rs_r.at[cid(p)], chip_dev(p))
    theirs = pl.ds(pl.multiple_of(o * HALF, 128), HALF)
    send("w", up_hbm.at[:, :, theirs], upv.at[:, units], w_s.at[0], w_r.at[0], sib)
    send("w", dn_hbm.at[:, :, theirs], dnv.at[:, units], w_s.at[1], w_r.at[1], sib)
    yown = jnp.concatenate([unit(pown.at[n], chip) for n in range(5)], axis=1)

    for n in range(4):
        part = pl.ds(n * 256, 256)
        v = lg[:, part]
        ex = jnp.exp(v - jnp.max(v, axis=0, keepdims=True))
        ex = ex / jnp.sum(ex, axis=0, keepdims=True)
        mxs[2 * n, all_rows, :] = ex[:, :128]
        mxs[2 * n + 1, all_rows, :] = ex[:, 128:]
    for n in range(8):
        part = pl.ds(n * 128, 128)
        rows = []
        for k in range(K):
            near = mxs[n, pl.ds(k, NZ, stride=K), :]
            far = mxs[n, pl.ds(NZ * K + k, NZ, stride=K), :]
            rows += [near[:4], far[:4], near[4:], far[4:]]
        mw[part, :] = jnp.concatenate(rows, axis=0).T.astype(BF)

    drain(("tab",))

    for p in CHIP_NEAR:
        arrived(cst.at[cid(p)], cst_s.at[cid(p)], cst_r.at[cid(p)])
    top = cst[0, 0]
    for j in range(1, NC):
        top = jnp.maximum(top, cst[j, 0])
    total = jnp.zeros((8, 128), F32)
    for j in range(NC):
        total += cst[j, 1] * jnp.exp(cst[j, 0] - top)
    row = lax.broadcasted_iota(jnp.int32, (8, 128), 0)
    factors = jnp.zeros((8, 128), F32)
    for j in range(NC):
        factors = jnp.where(row == j, jnp.exp(cst[j, 0] - top) / total, factors)
    fin[0:8, :] = factors
    ft[all_rows, :] = fin[...].T
    fk = unit(ft, chip)

    acc = yown * fk[:, 0:1]
    for p in CHIP_NEAR:
        j = cid(p)
        arrived(rs_recv.at[j], rs_s.at[j], rs_r.at[j])
        acc += rs_recv[j].astype(F32) * fk[:, j : j + 1]

    batch = lax.div(z, 4)
    place = batch * 8 + lax.rem(z, 4)
    a_send[...] = acc.reshape(NE, 1, HALF)
    for i in EXP_FAR:
        src = a_send.at[place_to(i)]
        there = place + 4 * i[0]
        send("a", src, a_recv.at[there], a_s.at[eid(i)], a_r.at[there], exp_dev(i))
    a_recv[place] = a_send[1]
    drain(("pp",))
    for c in loads[4:]:
        c.wait()
    arrived(upv.at[:, their_units], w_s.at[0], w_r.at[0])
    arrived(dnv.at[:, their_units], w_s.at[1], w_r.at[1])

    def rows_in(b):
        for n in range(8):
            wait = functools.partial(arrived, a_recv.at[b * 8 + n], a_s.at[0], a_r.at[b * 8 + n])
            if n < 4:
                pl.when(z != b * 4 + n)(wait)
            else:
                wait()
        xb[chip, b] = a_recv[pl.ds(b * 8, 8)].reshape(8, HALF).astype(BF)
        for p in CHIP_FAR:
            send("xg", xb.at[chip, b], xb.at[chip, b], xg_s.at[b, cid(p)], xg_r.at[b, cid(p)], chip_dev(p))

    def first(b, q):
        for p in ((q, 1), (q, 0)) if q else ((q, 1),):
            arrived(xb.at[chip_from(p), b], xg_s.at[b, cid(p)], xg_r.at[b, cid(p)])
        for n in range(2):
            k = chip_from((q, n))
            px_send[b, q, n, :, pl.ds(0, 2 * FD)] = nt(xb[k, b], upv[k])
        send("px", px_send.at[b, q], px_recv.at[b, q], px_s.at[b, q], px_r.at[b, q], sib)

    row8 = lax.broadcasted_iota(jnp.int32, (8, HALF), 0)

    def second(b, q):
        arrived(px_recv.at[b, q], px_s.at[b, q], px_r.at[b, q])
        both = []
        for n in range(2):
            k = chip_from((q, n))
            inner = px_send[b, q, n, :, pl.ds(0, 2 * FD)] + px_recv[b, q, n, :, pl.ds(0, 2 * FD)]
            both.append(mm(gelu(inner).astype(BF), dnv[k]))
        for n in range(2):
            value = jnp.where(row8 < 4, both[n], both[1 - n])
            if q or n:
                ro_send[b, q, n] = value.astype(BF)
                p = (4 - q if q else 0, n)
                sems = ro_s.at[b, cid(p)], ro_r.at[b, cid(p)]
                send("ro", ro_send.at[b, q, n], ro_recv.at[b, cid(p)], *sems, chip_dev(p))
            else:
                ro_own[b] = value

    def rows_out(b):
        total_b = ro_own[b]
        for p in CHIP_NEAR:
            arrived(ro_recv.at[b, cid(p)], ro_s.at[b, cid(p)], ro_r.at[b, cid(p)])
            total_b += ro_recv[b, cid(p)].astype(F32)
        b_send[pl.ds(b * 8, 8)] = total_b.reshape(8, 1, HALF)
        for turn in range(4):
            for rel in (1, 0):
                to_z = b * 4 + turn
                src = b_send.at[b * 8 + rel * 4 + turn]
                dev = ((flipped if rel else chip) * 2 + h, to_z * 2 + (1 - x_hi if rel else x_hi))
                u = lax.rem(z - to_z + 9, NZ)
                there = lax.div(u, 4) * 8 + rel * 4 + lax.rem(u, 4)
                c = copy(src, b_recv.at[there], b_s.at[b, rel * 4 + turn], b_r.at[there], dev)
                if rel:
                    c.start()
                else:
                    pl.when(z != to_z)(c.start)
        here = b * 8 + lax.rem(z, 4)

        @pl.when(batch == b)
        def _():
            b_recv[1] = b_send[here]

    def rows_out_done(b):
        for turn in range(4):
            for rel in range(2):
                c = copy(b_send.at[0], b_recv.at[0], b_s.at[b, rel * 4 + turn], b_r.at[0], sib)
                if rel:
                    c.wait_send()
                else:
                    pl.when(z != b * 4 + turn)(c.wait_send)

    def result_copies(g):
        mine = ret.at[h, chip, g]
        for target in [c * 2 + core for c in range(NC) for core in (1, 0)]:
            yield copy(mine, mine, rg_s.at[g, target], rg_r.at[g, h, chip], (target, e)), target

    def results(g):
        for c, target in result_copies(g):
            pl.when(target != s)(c.start)

    def own_clip(g):
        for j in range(g * 8, g * 8 + 8):
            if j != 1:
                arrived(b_recv.at[j], b_s.at[0, 0], b_r.at[j])
        ret[h, chip, g] = b_recv[pl.ds(g * 8, 8)].reshape(8, HALF).astype(BF)
        results(g)

    rows_in(0)
    rows_in(1)
    for q in (0, 1, 3, 2):
        first(0, q)
    for q in (0, 1, 3, 2):
        second(0, q)
    for q in (0, 1, 3, 2):
        first(1, q)
    for q in (0, 1, 3, 2):
        second(1, q)
    drain(("rs", "a", "w", "xg"))
    rows_out(0)
    rows_out(1)
    own_clip(0)
    own_clip(1)
    drain(("px", "ro"))
    rows_out_done(0)
    rows_out_done(1)
    for g in range(2):
        for p in CHIP_NEAR:
            arrived(ret.at[h, chip_from(p), g], rg_s.at[g, 0], rg_r.at[g, h, chip_from(p)])

    def mix(half):
        table = ret[half].astype(F32).reshape(SLOTS, HALF).astype(BF)
        lanes = pl.ds(pl.multiple_of(half * HALF, 128), HALF)
        for n in range(4):
            part = pl.ds(n * 256, 256)
            out_ref[part, lanes] = mm(mw[part, :], table).astype(BF)

    mix(h)
    for g in range(2):
        for p in ((0, 0),) + CHIP_NEAR:
            arrived(ret.at[o, chip_from(p), g], rg_s.at[g, 0], rg_r.at[g, o, chip_from(p)])
    mix(o)
    drain()
    for g in range(2):
        for c, target in result_copies(g):
            pl.when(target != s)(c.wait_send)


def shards(tokens, slot_params, up_weight, down_weight):
    vm = pltpu.VMEM
    dma = pltpu.SemaphoreType.DMA
    call = pl.pallas_call(
        kernel,
        out_shape=jax.ShapeDtypeStruct((ROWS, 2 * HALF), BF),
        in_specs=[pl.BlockSpec(memory_space=pltpu.HBM)] * 4,
        out_specs=pl.BlockSpec(memory_space=pltpu.VMEM),
        scratch_shapes=[
            vm((2, ROWS, HALF), BF),
            vm((K, 2 * FD, HALF), BF),
            vm((K, 2 * FD, HALF), BF),
            vm((2, NE, K, HALF), BF),
            vm((SLOTS, ROWS), F32),
            vm((SLOTS, ROWS), BF),
            vm((SLOTS, 128), F32),
            vm((2, 8, 128), F32),
            vm((2, 8, 128), F32),
            vm((NC, 2, 8, 128), F32),
            vm((128, 128), F32),
            vm((PADDED, 128), F32),
            vm((5, SLOTS, 128), F32),
            vm((5, PADDED, 128), F32),
            vm((5, SLOTS, 128), F32),
            vm((NC, NE, HALF), BF),
            vm((NC, NE, HALF), BF),
            vm((NE, 1, HALF), F32),
            vm((NE, 1, HALF), F32),
            vm((NC, 2, 8, HALF), BF),
            vm((2, 4, 2, 8, 384), F32),
            vm((2, 4, 2, 8, 384), F32),
            vm((2, 4, 2, 8, HALF), BF),
            vm((2, 8, HALF), F32),
            vm((2, NC, 8, HALF), BF),
            vm((NE, 1, HALF), F32),
            vm((NE, 1, HALF), F32),
            vm((2, NC, 2, 8, HALF), BF),
            vm((8, PADDED, 128), F32),
            vm((ROWS, SLOTS), BF),
            dma((8,)),
            dma((NE,)), dma((NE,)), dma((NE,)), dma((NE,)),
            dma, dma,
            dma((NC,)), dma((NC,)),
            dma((5,)), dma((5,)),
            dma((NC,)), dma((NC,)),
            dma((2,)), dma((2,)),
            dma((NE,)), dma((NE,)),
            dma((2, NC)), dma((2, NC)),
            dma((2, 4)), dma((2, 4)),
            dma((2, NC)), dma((2, NC)),
            dma((2, 8)), dma((NE,)),
            dma((2, 2 * NC)), dma((2, 2, NC)),
        ],
        compiler_params=pltpu.CompilerParams(
            collective_id=0, has_side_effects=True, vmem_limit_bytes=50 * 2**20
        ),
        cost_estimate=pl.CostEstimate(flops=1_400_000_000, bytes_accessed=14_000_000, transcendentals=400_000),
        name="soft_moe",
    )
    operands = (tokens.reshape(ROWS, 2 * HALF), slot_params.T, jnp.transpose(up_weight, (0, 2, 1)), down_weight)
    mixed = call(*(pltpu.with_memory_space_constraint(v, pltpu.HBM) for v in operands))
    return mixed.reshape(tokens.shape)


def solution(mesh):
    in_specs = (
        P("expert", "seq", None),
        P(None, "expert"),
        P("expert", None, "seq"),
        P("expert", "seq", None),
    )
    out_specs = P("expert", "seq", None)
    return jax.shard_map(shards, mesh=mesh, in_specs=in_specs, out_specs=out_specs, check_vma=False)
```

```python
import functools

import jax
import jax.numpy as jnp
from jax import lax
from jax.experimental import pallas as pl
from jax.experimental.pallas import tpu as pltpu
from jax.sharding import PartitionSpec as P

MESH = pl.DeviceIdType.MESH
BF = jnp.bfloat16
F32 = jnp.float32
NE = 16
NZ = 8
NC = 8
K = 8
HALF = 640
ROWS = 1024
FD = 160
SLOTS = NE * K
PADDED = SLOTS + 16

EXP_FAR = (
    (1, 4), (1, 3), (1, 5), (0, 4), (1, 2), (1, 6), (0, 3), (0, 5),
    (1, 1), (1, 7), (0, 2), (0, 6), (1, 0), (0, 1), (0, 7),
)
EXP_NEAR = tuple(reversed(EXP_FAR))
CHIP_FAR = ((2, 1), (2, 0), (1, 1), (3, 1), (1, 0), (3, 0), (0, 1))
CHIP_NEAR = tuple(reversed(CHIP_FAR))


def nt(a, b):
    return lax.dot_general(a, b, (((1,), (1,)), ((), ())), preferred_element_type=F32)


def mm(a, b):
    return jnp.dot(a, b, preferred_element_type=F32)


def gelu(v):
    return 0.5 * v * (1.0 + lax.erf(v * 0.7071067811865476))


def kernel(
    tok_hbm, sp_hbm, up_hbm, dn_hbm, out_ref,
    tokh, upv, dnv, tab, lg, wt, xs, stat, pst, cst, fin, ft,
    psend, pown, precv, rs_send, rs_recv, a_send, a_recv, xb,
    px_send, px_recv, ro_send, ro_own, ro_recv, b_send, b_recv, ret, mxs, mw,
    load_sem, tab_s, tab_r, tabf_s, tabf_r, pst_s, pst_r, cst_s, cst_r, pp_s, pp_r,
    rs_s, rs_r, w_s, w_r, a_s, a_r, xg_s, xg_r, px_s, px_r, ro_s, ro_r, b_s, b_r,
    rg_s, rg_r,
):
    s = lax.axis_index("seq")
    e = lax.axis_index("expert")
    chip = lax.div(s, 2)
    h = lax.rem(s, 2)
    o = 1 - h
    y = lax.div(chip, 2)
    x_lo = lax.rem(chip, 2)
    z = lax.div(e, 2)
    x_hi = lax.rem(e, 2)
    sib = (chip * 2 + o, e)
    flipped = y * 2 + 1 - x_lo

    def chip_at(p):
        return lax.rem(y + p[0], 4) * 2 + (1 - x_lo if p[1] else x_lo)

    def chip_from(p):
        return chip_at((4 - p[0], p[1]))

    def chip_dev(p):
        return (chip_at(p) * 2 + h, e)

    def exp_at(i):
        return lax.rem(z + i[1], NZ) * 2 + (1 - x_hi if i[0] else x_hi)

    def exp_dev(i):
        return ((flipped if i[0] else chip) * 2 + h, exp_at(i))

    def cid(p):
        return p[0] * 2 + p[1]

    def eid(i):
        return i[0] * NZ + i[1]

    def place_from(i):
        return i[0] * NZ + (1 - i[1]) % NZ

    live = []

    def drain(groups=None):
        for item in list(live):
            if groups is None or item[0] in groups:
                item[1].wait_send()
                live.remove(item)

    def copy(src, dst, ssem, rsem, dev):
        return pltpu.make_async_remote_copy(
            src_ref=src, dst_ref=dst, send_sem=ssem, recv_sem=rsem, device_id=dev, device_id_type=MESH
        )

    def send(group, src, dst, ssem, rsem, dev):
        c = copy(src, dst, ssem, rsem, dev)
        c.start()
        live.append((group, c))

    def arrived(dst, ssem, rsem):
        copy(dst, dst, ssem, rsem, sib).wait_recv()

    barrier = pltpu.get_barrier_semaphore()
    for i in EXP_FAR:
        pl.semaphore_signal(barrier, inc=1, device_id=exp_dev(i), device_id_type=MESH)
    for p in CHIP_FAR:
        pl.semaphore_signal(barrier, inc=1, device_id=chip_dev(p), device_id_type=MESH)
    for p in CHIP_FAR:
        pl.semaphore_signal(barrier, inc=1, device_id=(chip_at(p) * 2 + o, e), device_id_type=MESH)
    pl.semaphore_signal(barrier, inc=1, device_id=sib, device_id_type=MESH)

    loads = []
    for half in range(2):
        lanes = pl.ds(half * HALF, HALF)
        c = pltpu.make_async_copy(sp_hbm.at[:, lanes], tab.at[half, 1], load_sem.at[4 + half])
        c.start()
        loads.append(c)
    for half in range(2):
        c = pltpu.make_async_copy(tok_hbm.at[:, pl.ds(half * HALF, HALF)], tokh.at[half], load_sem.at[half])
        c.start()
        loads.append(c)
    ours = pl.ds(pl.multiple_of(h * HALF, 128), HALF)
    units = pl.ds(pl.multiple_of(h * FD, 16), FD)
    their_units = pl.ds(pl.multiple_of(o * FD, 16), FD)
    for n, (src, dst) in enumerate(((up_hbm, upv), (dn_hbm, dnv))):
        c = pltpu.make_async_copy(src.at[:, :, ours], dst.at[:, units], load_sem.at[2 + n])
        c.start()
        loads.append(c)
    fin[...] = jnp.zeros_like(fin)
    px_send[...] = jnp.zeros_like(px_send)
    loads[0].wait()
    loads[1].wait()
    pl.semaphore_wait(barrier, NE - 1 + 2 * (NC - 1) + 1)

    for i in EXP_FAR:
        send("tab", tab.at[h, 1], tab.at[h, place_from(i)], tab_s.at[eid(i)], tab_r.at[eid(i)], exp_dev(i))
    for i in EXP_NEAR:
        src = tab.at[h, place_from(i)]
        arrived(src, tab_s.at[eid(i)], tab_r.at[eid(i)])
        send("tab", src, src, tabf_s.at[eid(i)], tabf_r, sib)
    loads[2].wait()
    loads[3].wait()
    half_table = tab[h].astype(F32).reshape(SLOTS, HALF).astype(BF)
    for n in range(4):
        part = pl.ds(n * 256, 256)
        lg[:, part] = nt(half_table, tokh[h, part, :])
    arrived(tab.at[o, pl.ds(0, NE - 1)], tabf_s.at[0], tabf_r)
    half_table = tab[o].astype(F32).reshape(SLOTS, HALF).astype(BF)
    for n in range(4):
        part = pl.ds(n * 256, 256)
        lg[:, part] += nt(half_table, tokh[o, part, :])

    lane = lax.broadcasted_iota(jnp.int32, (32, 128), 1)
    for r in range(0, SLOTS, 32):
        part = pl.ds(r, 32)
        v = lg[part, :]
        m = jnp.max(v, axis=1, keepdims=True)
        ex = jnp.exp(v - m)
        l = jnp.sum(ex, axis=1, keepdims=True)
        wt[part, :] = ex.astype(BF)
        xs[part, :] = jnp.where(lane < 64, m, l)
    xt = xs[...].T
    m0 = jnp.broadcast_to(xt[0:1, :], (8, 128))
    l0 = jnp.broadcast_to(xt[64:65, :], (8, 128))
    stat[0] = m0
    stat[1] = l0
    send("tab", stat, pst, pst_s, pst_r, sib)

    for n, w in ((0, 2), (2, 2), (4, 1)):
        sums = mm(wt[...], tokh[o, :, pl.ds(n * 128, w * 128)])
        for q in range(w):
            psend[n + q] = sums[:, q * 128 : q * 128 + 128]
        part = pl.ds(n, w)
        send("pp", psend.at[part], precv.at[part], pp_s.at[n], pp_r.at[n], sib)
    sums = mm(wt[...], tokh[h])
    all_rows = pl.ds(0, SLOTS)
    for n in range(5):
        pown[n, all_rows, :] = sums[:, n * 128 : n * 128 + 128]
    arrived(pst, pst_s, pst_r)
    m1 = pst[0]
    mc = jnp.maximum(m0, m1)
    g0 = jnp.exp(m0 - mc)
    g1 = jnp.exp(m1 - mc)
    cst[0, 0] = mc
    cst[0, 1] = l0 * g0 + pst[1] * g1
    for p in CHIP_FAR:
        send("pp", cst.at[0], cst.at[cid(p)], cst_s.at[cid(p)], cst_r, chip_dev(p))
    scale0 = jnp.broadcast_to(g0[0:1, :], (128, 128)).T
    scale1 = jnp.broadcast_to(g1[0:1, :], (128, 128)).T

    def unit(ref, k):
        near = ref[pl.ds(k, NZ, stride=K), :]
        far = ref[pl.ds(NZ * K + k + 1 - 2 * lax.rem(k, 2), NZ, stride=K), :]
        return jnp.concatenate([near[:4], far[:4], near[4:], far[4:]], axis=0)

    def sums_to(g, p):
        j = cid(p)
        send("rs", rs_send.at[g, j], rs_recv.at[g, j], rs_s.at[g, j], rs_r.at[g], chip_dev(p))

    for n, w in ((0, 2), (2, 2), (4, 1)):
        arrived(precv.at[pl.ds(n, w)], pp_s.at[n], pp_r.at[n])
        for q in range(n, n + w):
            pown[q, all_rows, :] = pown[q, all_rows, :] * scale0 + precv[q] * scale1
    for p in CHIP_FAR:
        for n in range(5):
            rows = unit(pown.at[n], chip_at(p))
            for g in range(2):
                rs_send[g, cid(p), :, pl.ds(n * 128, 128)] = rows[g * 8 : g * 8 + 8].astype(BF)
        sums_to(1, p)
    for p in CHIP_FAR:
        sums_to(0, p)
    theirs = pl.ds(pl.multiple_of(o * HALF, 128), HALF)
    send("w", up_hbm.at[:, :, theirs], upv.at[:, units], w_s.at[0], w_r.at[0], sib)
    send("w", dn_hbm.at[:, :, theirs], dnv.at[:, units], w_s.at[1], w_r.at[1], sib)
    yown = jnp.concatenate([unit(pown.at[n], chip) for n in range(5)], axis=1)

    for n in range(4):
        part = pl.ds(n * 256, 256)
        v = lg[:, part]
        ex = jnp.exp(v - jnp.max(v, axis=0, keepdims=True))
        ex = ex / jnp.sum(ex, axis=0, keepdims=True)
        mxs[2 * n, all_rows, :] = ex[:, :128]
        mxs[2 * n + 1, all_rows, :] = ex[:, 128:]
    for n in range(8):
        part = pl.ds(n * 128, 128)
        rows = []
        for k in range(K):
            near = mxs[n, pl.ds(k, NZ, stride=K), :]
            far = mxs[n, pl.ds(NZ * K + k, NZ, stride=K), :]
            rows += [near[:4], far[:4], near[4:], far[4:]]
        mw[part, :] = jnp.concatenate(rows, axis=0).T.astype(BF)

    drain(("tab",))

    arrived(cst.at[pl.ds(1, NC - 1)], cst_s.at[0], cst_r)
    top = cst[0, 0]
    for j in range(1, NC):
        top = jnp.maximum(top, cst[j, 0])
    total = jnp.zeros((8, 128), F32)
    for j in range(NC):
        total += cst[j, 1] * jnp.exp(cst[j, 0] - top)
    row = lax.broadcasted_iota(jnp.int32, (8, 128), 0)
    factors = jnp.zeros((8, 128), F32)
    for j in range(NC):
        factors = jnp.where(row == j, jnp.exp(cst[j, 0] - top) / total, factors)
    fin[0:8, :] = factors
    ft[all_rows, :] = fin[...].T
    fk = unit(ft, chip)

    batch = lax.div(z, 4)
    place = batch * 8 + lax.rem(z, 4)
    for g in (1, 0):
        rows = slice(g * 8, g * 8 + 8)
        acc = yown[rows] * fk[rows, 0:1]
        arrived(rs_recv.at[g, pl.ds(1, NC - 1)], rs_s.at[g, 0], rs_r.at[g])
        for j in range(1, NC):
            acc += rs_recv[g, j].astype(F32) * fk[rows, j : j + 1]
        a_send[pl.ds(g * 8, 8)] = acc.reshape(8, 1, HALF)
        for i in EXP_FAR:
            u = (i[1] + 1) % NZ
            if u // 4 == g:
                src = a_send.at[g * 8 + i[0] * 4 + u % 4]
                there = place + 4 * i[0]
                send("a", src, a_recv.at[there], a_s.at[eid(i)], a_r.at[batch], exp_dev(i))
    a_recv[place] = a_send[1]
    drain(("pp",))
    for c in loads[4:]:
        c.wait()
    arrived(upv.at[:, their_units], w_s.at[0], w_r.at[0])
    arrived(dnv.at[:, their_units], w_s.at[1], w_r.at[1])

    def rows_in(b):
        for others, here in ((7, batch == b), (8, batch != b)):
            wait = functools.partial(arrived, a_recv.at[pl.ds(b * 8, others)], a_s.at[0], a_r.at[b])
            pl.when(here)(wait)
        xb[chip, b] = a_recv[pl.ds(b * 8, 8)].reshape(8, HALF).astype(BF)
        for p in CHIP_FAR:
            send("xg", xb.at[chip, b], xb.at[chip, b], xg_s.at[b, cid(p)], xg_r.at[b, cid(p)], chip_dev(p))

    def first(b, q):
        for p in ((q, 1), (q, 0)) if q else ((q, 1),):
            arrived(xb.at[chip_from(p), b], xg_s.at[b, cid(p)], xg_r.at[b, cid(p)])
        for n in range(2):
            k = chip_from((q, n))
            px_send[b, q, n, :, pl.ds(0, 2 * FD)] = nt(xb[k, b], upv[k])
        send("px", px_send.at[b, q], px_recv.at[b, q], px_s.at[b, q], px_r.at[b, q], sib)

    row8 = lax.broadcasted_iota(jnp.int32, (8, HALF), 0)

    def second(b, q):
        arrived(px_recv.at[b, q], px_s.at[b, q], px_r.at[b, q])
        both = []
        for n in range(2):
            k = chip_from((q, n))
            inner = px_send[b, q, n, :, pl.ds(0, 2 * FD)] + px_recv[b, q, n, :, pl.ds(0, 2 * FD)]
            both.append(mm(gelu(inner).astype(BF), dnv[k]))
        for n in range(2):
            value = jnp.where(row8 < 4, both[n], both[1 - n])
            if q or n:
                ro_send[b, q, n] = value.astype(BF)
                p = (4 - q if q else 0, n)
                sems = ro_s.at[b, cid(p)], ro_r.at[b]
                send("ro", ro_send.at[b, q, n], ro_recv.at[b, cid(p)], *sems, chip_dev(p))
            else:
                ro_own[b] = value

    def rows_out(b):
        total_b = ro_own[b]
        arrived(ro_recv.at[b, pl.ds(1, NC - 1)], ro_s.at[b, 0], ro_r.at[b])
        for j in range(1, NC):
            total_b += ro_recv[b, j].astype(F32)
        b_send[pl.ds(b * 8, 8)] = total_b.reshape(8, 1, HALF)
        for turn in range(4):
            for rel in (1, 0):
                to_z = b * 4 + turn
                src = b_send.at[b * 8 + rel * 4 + turn]
                dev = ((flipped if rel else chip) * 2 + h, to_z * 2 + (1 - x_hi if rel else x_hi))
                u = lax.rem(z - to_z + 9, NZ)
                there = lax.div(u, 4) * 8 + rel * 4 + lax.rem(u, 4)
                c = copy(src, b_recv.at[there], b_s.at[b, rel * 4 + turn], b_r.at[lax.div(u, 4)], dev)
                if rel:
                    c.start()
                else:
                    pl.when(z != to_z)(c.start)
        here = b * 8 + lax.rem(z, 4)

        @pl.when(batch == b)
        def _():
            b_recv[1] = b_send[here]

    def rows_out_done(b):
        for turn in range(4):
            for rel in range(2):
                c = copy(b_send.at[0], b_recv.at[0], b_s.at[b, rel * 4 + turn], b_r.at[0], sib)
                if rel:
                    c.wait_send()
                else:
                    pl.when(z != b * 4 + turn)(c.wait_send)

    def result_copies(g):
        mine = ret.at[h, chip, g]
        for target in [c * 2 + core for c in range(NC) for core in (1, 0)]:
            yield copy(mine, mine, rg_s.at[g], rg_r.at[g, h], (target, e)), target

    def results(g):
        for c, target in result_copies(g):
            pl.when(target != s)(c.start)

    def own_clip(g):
        arrived(b_recv.at[pl.ds(g * 8, 7 + g)], b_s.at[0, 0], b_r.at[g])
        ret[h, chip, g] = b_recv[pl.ds(g * 8, 8)].reshape(8, HALF).astype(BF)
        results(g)

    rows_in(0)
    rows_in(1)
    for q in (0, 1, 3, 2):
        first(0, q)
    for q in (0, 1, 3, 2):
        second(0, q)
    for q in (0, 1, 3, 2):
        first(1, q)
    for q in (0, 1, 3, 2):
        second(1, q)
    drain(("rs", "a", "w", "xg"))
    rows_out(0)
    rows_out(1)
    own_clip(0)
    own_clip(1)
    drain(("px", "ro"))
    rows_out_done(0)
    rows_out_done(1)
    for g in range(2):
        arrived(tab.at[0, pl.ds(0, NC - 1)], rg_s.at[g], rg_r.at[g, h])

    def mix(half):
        table = ret[half].astype(F32).reshape(SLOTS, HALF).astype(BF)
        lanes = pl.ds(pl.multiple_of(half * HALF, 128), HALF)
        for n in range(4):
            part = pl.ds(n * 256, 256)
            out_ref[part, lanes] = mm(mw[part, :], table).astype(BF)

    mix(h)
    for g in range(2):
        arrived(tab.at[0, pl.ds(0, NC)], rg_s.at[g], rg_r.at[g, o])
    mix(o)
    drain()
    for g in range(2):
        block = tab.at[0, pl.ds(0, 2 * NC - 1)]
        copy(block, block, rg_s.at[g], rg_r.at[g, 0], sib).wait_send()


def shards(tokens, slot_params, up_weight, down_weight):
    vm = pltpu.VMEM
    dma = pltpu.SemaphoreType.DMA
    call = pl.pallas_call(
        kernel,
        out_shape=jax.ShapeDtypeStruct((ROWS, 2 * HALF), BF),
        in_specs=[pl.BlockSpec(memory_space=pltpu.HBM)] * 4,
        out_specs=pl.BlockSpec(memory_space=pltpu.VMEM),
        scratch_shapes=[
            vm((2, ROWS, HALF), BF),
            vm((K, 2 * FD, HALF), BF),
            vm((K, 2 * FD, HALF), BF),
            vm((2, NE, K, HALF), BF),
            vm((SLOTS, ROWS), F32),
            vm((SLOTS, ROWS), BF),
            vm((SLOTS, 128), F32),
            vm((2, 8, 128), F32),
            vm((2, 8, 128), F32),
            vm((NC, 2, 8, 128), F32),
            vm((128, 128), F32),
            vm((PADDED, 128), F32),
            vm((5, SLOTS, 128), F32),
            vm((5, PADDED, 128), F32),
            vm((5, SLOTS, 128), F32),
            vm((2, NC, 8, HALF), BF),
            vm((2, NC, 8, HALF), BF),
            vm((NE, 1, HALF), F32),
            vm((NE, 1, HALF), F32),
            vm((NC, 2, 8, HALF), BF),
            vm((2, 4, 2, 8, 384), F32),
            vm((2, 4, 2, 8, 384), F32),
            vm((2, 4, 2, 8, HALF), BF),
            vm((2, 8, HALF), F32),
            vm((2, NC, 8, HALF), BF),
            vm((NE, 1, HALF), F32),
            vm((NE, 1, HALF), F32),
            vm((2, NC, 2, 8, HALF), BF),
            vm((8, PADDED, 128), F32),
            vm((ROWS, SLOTS), BF),
            dma((8,)),
            dma((NE,)), dma((NE,)), dma((NE,)), dma,
            dma, dma,
            dma((NC,)), dma,
            dma((5,)), dma((5,)),
            dma((2, NC)), dma((2,)),
            dma((2,)), dma((2,)),
            dma((NE,)), dma((2,)),
            dma((2, NC)), dma((2, NC)),
            dma((2, 4)), dma((2, 4)),
            dma((2, NC)), dma((2,)),
            dma((2, 8)), dma((2,)),
            dma((2,)), dma((2, 2)),
        ],
        compiler_params=pltpu.CompilerParams(
            collective_id=0, has_side_effects=True, vmem_limit_bytes=50 * 2**20
        ),
        cost_estimate=pl.CostEstimate(flops=1_400_000_000, bytes_accessed=14_000_000, transcendentals=400_000),
        name="soft_moe",
    )
    operands = (tokens.reshape(ROWS, 2 * HALF), slot_params.T, jnp.transpose(up_weight, (0, 2, 1)), down_weight)
    mixed = call(*(pltpu.with_memory_space_constraint(v, pltpu.HBM) for v in operands))
    return mixed.reshape(tokens.shape)


def solution(mesh):
    in_specs = (
        P("expert", "seq", None),
        P(None, "expert"),
        P("expert", None, "seq"),
        P("expert", "seq", None),
    )
    out_specs = P("expert", "seq", None)
    return jax.shard_map(shards, mesh=mesh, in_specs=in_specs, out_specs=out_specs, check_vma=False)
```

```python
import functools

import jax
import jax.numpy as jnp
from jax import lax
from jax.experimental import pallas as pl
from jax.experimental.pallas import tpu as pltpu
from jax.sharding import PartitionSpec as P

MESH = pl.DeviceIdType.MESH
BF = jnp.bfloat16
F32 = jnp.float32
NE = 16
NZ = 8
NC = 8
K = 8
HALF = 640
ROWS = 1024
FD = 160
SLOTS = NE * K
PADDED = SLOTS + 16

EXP_FAR = (
    (1, 4), (1, 3), (1, 5), (0, 4), (1, 2), (1, 6), (0, 3), (0, 5),
    (1, 1), (1, 7), (0, 2), (0, 6), (1, 0), (0, 1), (0, 7),
)
EXP_NEAR = tuple(reversed(EXP_FAR))
CHIP_FAR = ((2, 1), (2, 0), (1, 1), (3, 1), (1, 0), (3, 0), (0, 1))
CHIP_NEAR = tuple(reversed(CHIP_FAR))


def nt(a, b):
    return lax.dot_general(a, b, (((1,), (1,)), ((), ())), preferred_element_type=F32)


def mm(a, b):
    return jnp.dot(a, b, preferred_element_type=F32)


def gelu(v):
    return 0.5 * v * (1.0 + lax.erf(v * 0.7071067811865476))


def kernel(
    tok_hbm, sp_hbm, up_hbm, dn_hbm, out_ref,
    tokh, upv, dnv, tab, lg, wt, xs, stat, pst, cst, fin, ft,
    psend, pown, precv, rs_send, rs_recv, a_send, a_recv, xb,
    px_send, px_recv, ro_send, ro_own, ro_recv, b_send, b_recv, ret, mxs, mw,
    load_sem, tab_s, tab_r, tabf_s, tabf_r, pst_s, pst_r, cst_s, cst_r, pp_s, pp_r,
    rs_s, rs_r, w_s, w_r, a_s, a_r, xg_s, xg_r, px_s, px_r, ro_s, ro_r, b_s, b_r,
    rg_s, rg_r,
):
    s = lax.axis_index("seq")
    e = lax.axis_index("expert")
    chip = lax.div(s, 2)
    h = lax.rem(s, 2)
    o = 1 - h
    y = lax.div(chip, 2)
    x_lo = lax.rem(chip, 2)
    z = lax.div(e, 2)
    x_hi = lax.rem(e, 2)
    sib = (chip * 2 + o, e)
    flipped = y * 2 + 1 - x_lo

    def chip_at(p):
        return lax.rem(y + p[0], 4) * 2 + (1 - x_lo if p[1] else x_lo)

    def chip_from(p):
        return chip_at((4 - p[0], p[1]))

    def chip_dev(p):
        return (chip_at(p) * 2 + h, e)

    def exp_at(i):
        return lax.rem(z + i[1], NZ) * 2 + (1 - x_hi if i[0] else x_hi)

    def exp_dev(i):
        return ((flipped if i[0] else chip) * 2 + h, exp_at(i))

    def cid(p):
        return p[0] * 2 + p[1]

    def eid(i):
        return i[0] * NZ + i[1]

    def place_from(i):
        return i[0] * NZ + (1 - i[1]) % NZ

    def copy(src, dst, ssem, rsem, dev):
        return pltpu.make_async_remote_copy(
            src_ref=src, dst_ref=dst, send_sem=ssem, recv_sem=rsem, device_id=dev, device_id_type=MESH
        )

    def send(src, dst, ssem, rsem, dev):
        copy(src, dst, ssem, rsem, dev).start()

    def sent(ref, ssem):
        copy(ref, ref, ssem, ssem, sib).wait_send()

    def blocks(n):
        return tab.at[0, pl.ds(0, n)]

    def arrived(dst, ssem, rsem):
        copy(dst, dst, ssem, rsem, sib).wait_recv()

    barrier = pltpu.get_barrier_semaphore()
    for i in EXP_FAR:
        pl.semaphore_signal(barrier, inc=1, device_id=exp_dev(i), device_id_type=MESH)
    for p in CHIP_FAR:
        pl.semaphore_signal(barrier, inc=1, device_id=chip_dev(p), device_id_type=MESH)
    for p in CHIP_FAR:
        pl.semaphore_signal(barrier, inc=1, device_id=(chip_at(p) * 2 + o, e), device_id_type=MESH)
    pl.semaphore_signal(barrier, inc=1, device_id=sib, device_id_type=MESH)

    loads = []
    ours = pl.ds(pl.multiple_of(h * HALF, 128), HALF)
    c = pltpu.make_async_copy(sp_hbm.at[:, ours], tab.at[h, 1], load_sem.at[4])
    c.start()
    loads.append(c)
    for half in range(2):
        c = pltpu.make_async_copy(tok_hbm.at[:, pl.ds(half * HALF, HALF)], tokh.at[half], load_sem.at[half])
        c.start()
        loads.append(c)
    units = pl.ds(pl.multiple_of(h * FD, 16), FD)
    their_units = pl.ds(pl.multiple_of(o * FD, 16), FD)
    for n, (src, dst) in enumerate(((up_hbm, upv), (dn_hbm, dnv))):
        c = pltpu.make_async_copy(src.at[:, :, ours], dst.at[:, units], load_sem.at[2 + n])
        c.start()
        loads.append(c)
    fin[...] = jnp.zeros_like(fin)
    px_send[...] = jnp.zeros_like(px_send)
    loads[0].wait()
    pl.semaphore_wait(barrier, NE - 1 + 2 * (NC - 1) + 1)

    for i in EXP_FAR:
        send(tab.at[h, 1], tab.at[h, place_from(i)], tab_s, tab_r.at[place_from(i) // 4], exp_dev(i))
    for g in (0, 2, 1, 3):
        arrived(blocks(4 if g else 3), tab_s, tab_r.at[g])
        four = tab.at[h, pl.ds(4 * g, 4)]
        send(four, four, tabf_s, tabf_r, sib)
    loads[1].wait()
    loads[2].wait()
    half_table = tab[h].astype(F32).reshape(SLOTS, HALF).astype(BF)
    for n in range(4):
        part = pl.ds(n * 256, 256)
        lg[:, part] = nt(half_table, tokh[h, part, :])
    arrived(tab.at[o], tabf_s, tabf_r)
    half_table = tab[o].astype(F32).reshape(SLOTS, HALF).astype(BF)
    for n in range(4):
        part = pl.ds(n * 256, 256)
        lg[:, part] += nt(half_table, tokh[o, part, :])

    lane = lax.broadcasted_iota(jnp.int32, (32, 128), 1)
    for r in range(0, SLOTS, 32):
        part = pl.ds(r, 32)
        v = lg[part, :]
        m = jnp.max(v, axis=1, keepdims=True)
        ex = jnp.exp(v - m)
        l = jnp.sum(ex, axis=1, keepdims=True)
        wt[part, :] = ex.astype(BF)
        xs[part, :] = jnp.where(lane < 64, m, l)
    xt = xs[...].T
    m0 = jnp.broadcast_to(xt[0:1, :], (8, 128))
    l0 = jnp.broadcast_to(xt[64:65, :], (8, 128))
    stat[0] = m0
    stat[1] = l0
    send(stat, pst, pst_s, pst_r, sib)

    for n, w in ((0, 2), (2, 2), (4, 1)):
        sums = mm(wt[...], tokh[o, :, pl.ds(n * 128, w * 128)])
        for q in range(w):
            psend[n + q] = sums[:, q * 128 : q * 128 + 128]
        part = pl.ds(n, w)
        send(psend.at[part], precv.at[part], pp_s, pp_r.at[n], sib)
    sums = mm(wt[...], tokh[h])
    all_rows = pl.ds(0, SLOTS)
    for n in range(5):
        pown[n, all_rows, :] = sums[:, n * 128 : n * 128 + 128]
    arrived(pst, pst_s, pst_r)
    m1 = pst[0]
    mc = jnp.maximum(m0, m1)
    g0 = jnp.exp(m0 - mc)
    g1 = jnp.exp(m1 - mc)
    cst[0, 0] = mc
    cst[0, 1] = l0 * g0 + pst[1] * g1
    for p in CHIP_FAR:
        send(cst.at[0], cst.at[cid(p)], cst_s, cst_r, chip_dev(p))
    scale0 = jnp.broadcast_to(g0[0:1, :], (128, 128)).T
    scale1 = jnp.broadcast_to(g1[0:1, :], (128, 128)).T

    def unit(ref, k):
        near = ref[pl.ds(k, NZ, stride=K), :]
        far = ref[pl.ds(NZ * K + k + 1 - 2 * lax.rem(k, 2), NZ, stride=K), :]
        return jnp.concatenate([near[:4], far[:4], near[4:], far[4:]], axis=0)

    def sums_to(g, p):
        j = cid(p)
        send(rs_send.at[g, j], rs_recv.at[g, j], rs_s, rs_r.at[g], chip_dev(p))

    for n, w in ((0, 2), (2, 2), (4, 1)):
        arrived(precv.at[pl.ds(n, w)], pp_s, pp_r.at[n])
        for q in range(n, n + w):
            pown[q, all_rows, :] = pown[q, all_rows, :] * scale0 + precv[q] * scale1
    for p in CHIP_FAR:
        for n in range(5):
            rows = unit(pown.at[n], chip_at(p))
            for g in range(2):
                rs_send[g, cid(p), :, pl.ds(n * 128, 128)] = rows[g * 8 : g * 8 + 8].astype(BF)
        sums_to(1, p)
    for p in CHIP_FAR:
        sums_to(0, p)
    theirs = pl.ds(pl.multiple_of(o * HALF, 128), HALF)
    send(up_hbm.at[:, :, theirs], upv.at[:, units], w_s.at[0], w_r.at[0], sib)
    send(dn_hbm.at[:, :, theirs], dnv.at[:, units], w_s.at[1], w_r.at[1], sib)
    yown = jnp.concatenate([unit(pown.at[n], chip) for n in range(5)], axis=1)

    for n in range(4):
        part = pl.ds(n * 256, 256)
        v = lg[:, part]
        ex = jnp.exp(v - jnp.max(v, axis=0, keepdims=True))
        ex = ex / jnp.sum(ex, axis=0, keepdims=True)
        mxs[2 * n, all_rows, :] = ex[:, :128]
        mxs[2 * n + 1, all_rows, :] = ex[:, 128:]
    for n in range(8):
        part = pl.ds(n * 128, 128)
        rows = []
        for k in range(K):
            near = mxs[n, pl.ds(k, NZ, stride=K), :]
            far = mxs[n, pl.ds(NZ * K + k, NZ, stride=K), :]
            rows += [near[:4], far[:4], near[4:], far[4:]]
        mw[part, :] = jnp.concatenate(rows, axis=0).T.astype(BF)

    sent(blocks(NE - 1), tab_s)
    sent(tab.at[h], tabf_s)
    sent(stat, pst_s)

    arrived(cst.at[pl.ds(1, NC - 1)], cst_s, cst_r)
    top = cst[0, 0]
    for j in range(1, NC):
        top = jnp.maximum(top, cst[j, 0])
    total = jnp.zeros((8, 128), F32)
    for j in range(NC):
        total += cst[j, 1] * jnp.exp(cst[j, 0] - top)
    row = lax.broadcasted_iota(jnp.int32, (8, 128), 0)
    factors = jnp.zeros((8, 128), F32)
    for j in range(NC):
        factors = jnp.where(row == j, jnp.exp(cst[j, 0] - top) / total, factors)
    fin[0:8, :] = factors
    ft[all_rows, :] = fin[...].T
    fk = unit(ft, chip)

    batch = lax.div(z, 4)
    place = batch * 8 + lax.rem(z, 4)
    for g in (1, 0):
        rows = slice(g * 8, g * 8 + 8)
        acc = yown[rows] * fk[rows, 0:1]
        arrived(rs_recv.at[g, pl.ds(1, NC - 1)], rs_s, rs_r.at[g])
        for j in range(1, NC):
            acc += rs_recv[g, j].astype(F32) * fk[rows, j : j + 1]
        a_send[pl.ds(g * 8, 8)] = acc.reshape(8, 1, HALF)
        for i in EXP_FAR:
            u = (i[1] + 1) % NZ
            if u // 4 == g:
                src = a_send.at[g * 8 + i[0] * 4 + u % 4]
                there = place + 4 * i[0]
                send(src, a_recv.at[there], a_s, a_r.at[batch], exp_dev(i))
    a_recv[place] = a_send[1]
    sent(psend, pp_s)
    sent(cst.at[pl.ds(1, NC - 1)], cst_s)
    for c in loads[3:]:
        c.wait()
    arrived(upv.at[:, their_units], w_s.at[0], w_r.at[0])
    arrived(dnv.at[:, their_units], w_s.at[1], w_r.at[1])

    def rows_in(b):
        for others, here in ((7, batch == b), (8, batch != b)):
            wait = functools.partial(arrived, a_recv.at[pl.ds(b * 8, others)], a_s, a_r.at[b])
            pl.when(here)(wait)
        xb[chip, b] = a_recv[pl.ds(b * 8, 8)].reshape(8, HALF).astype(BF)
        for p in CHIP_FAR:
            send(xb.at[chip, b], xb.at[chip, b], xg_s, xg_r.at[b, p[0]], chip_dev(p))

    def first(b, q):
        arrived(blocks(2 if q else 1), xg_s, xg_r.at[b, q])
        for n in range(2):
            k = chip_from((q, n))
            px_send[b, q, n, :, pl.ds(0, 2 * FD)] = nt(xb[k, b], upv[k])
        send(px_send.at[b, q], px_recv.at[b, q], px_s, px_r.at[b, q], sib)

    row8 = lax.broadcasted_iota(jnp.int32, (8, HALF), 0)

    def second(b, q):
        arrived(px_recv.at[b, q], px_s, px_r.at[b, q])
        both = []
        for n in range(2):
            k = chip_from((q, n))
            inner = px_send[b, q, n, :, pl.ds(0, 2 * FD)] + px_recv[b, q, n, :, pl.ds(0, 2 * FD)]
            both.append(mm(gelu(inner).astype(BF), dnv[k]))
        for n in range(2):
            value = jnp.where(row8 < 4, both[n], both[1 - n])
            if q or n:
                ro_send[b, q, n] = value.astype(BF)
                p = (4 - q if q else 0, n)
                sems = ro_s, ro_r.at[b]
                send(ro_send.at[b, q, n], ro_recv.at[b, cid(p)], *sems, chip_dev(p))
            else:
                ro_own[b] = value

    def rows_out(b):
        total_b = ro_own[b]
        arrived(ro_recv.at[b, pl.ds(1, NC - 1)], ro_s, ro_r.at[b])
        for j in range(1, NC):
            total_b += ro_recv[b, j].astype(F32)
        b_send[pl.ds(b * 8, 8)] = total_b.reshape(8, 1, HALF)
        for turn in range(4):
            for rel in (1, 0):
                to_z = b * 4 + turn
                src = b_send.at[b * 8 + rel * 4 + turn]
                dev = ((flipped if rel else chip) * 2 + h, to_z * 2 + (1 - x_hi if rel else x_hi))
                u = lax.rem(z - to_z + 9, NZ)
                there = lax.div(u, 4) * 8 + rel * 4 + lax.rem(u, 4)
                c = copy(src, b_recv.at[there], b_s, b_r.at[lax.div(u, 4)], dev)
                if rel:
                    c.start()
                else:
                    pl.when(z != to_z)(c.start)
        here = b * 8 + lax.rem(z, 4)

        @pl.when(batch == b)
        def _():
            b_recv[1] = b_send[here]

    def result_copies(g):
        mine = ret.at[h, chip, g]
        for target in [c * 2 + core for c in range(NC) for core in (1, 0)]:
            yield copy(mine, mine, rg_s.at[g], rg_r.at[g, h], (target, e)), target

    def results(g):
        for c, target in result_copies(g):
            pl.when(target != s)(c.start)

    def own_clip(g):
        arrived(b_recv.at[pl.ds(g * 8, 7 + g)], b_s, b_r.at[g])
        ret[h, chip, g] = b_recv[pl.ds(g * 8, 8)].reshape(8, HALF).astype(BF)
        results(g)

    rows_in(0)
    rows_in(1)
    for q in (0, 1, 3, 2):
        first(0, q)
    for q in (0, 1, 3, 2):
        second(0, q)
    for q in (0, 1, 3, 2):
        first(1, q)
    for q in (0, 1, 3, 2):
        second(1, q)
    sent(blocks(2 * NC - 2), rs_s)
    sent(a_recv.at[pl.ds(0, NE - 1)], a_s)
    sent(blocks(2 * NC - 2), xg_s)
    sent(upv.at[:, units], w_s.at[0])
    sent(dnv.at[:, units], w_s.at[1])
    rows_out(0)
    rows_out(1)
    own_clip(0)
    own_clip(1)
    sent(px_send, px_s)
    sent(blocks(2 * NC - 2), ro_s)
    sent(b_recv.at[pl.ds(0, NE - 1)], b_s)
    for g in range(2):
        arrived(blocks(NC - 1), rg_s.at[g], rg_r.at[g, h])

    def mix(half):
        table = ret[half].astype(F32).reshape(SLOTS, HALF).astype(BF)
        lanes = pl.ds(pl.multiple_of(half * HALF, 128), HALF)
        for n in range(4):
            part = pl.ds(n * 256, 256)
            out_ref[part, lanes] = mm(mw[part, :], table).astype(BF)

    mix(h)
    for g in range(2):
        arrived(blocks(NC), rg_s.at[g], rg_r.at[g, o])
    mix(o)
    for g in range(2):
        sent(blocks(2 * NC - 1), rg_s.at[g])


def shards(tokens, slot_params, up_weight, down_weight):
    vm = pltpu.VMEM
    dma = pltpu.SemaphoreType.DMA
    call = pl.pallas_call(
        kernel,
        out_shape=jax.ShapeDtypeStruct((ROWS, 2 * HALF), BF),
        in_specs=[pl.BlockSpec(memory_space=pltpu.HBM)] * 4,
        out_specs=pl.BlockSpec(memory_space=pltpu.VMEM),
        scratch_shapes=[
            vm((2, ROWS, HALF), BF),
            vm((K, 2 * FD, HALF), BF),
            vm((K, 2 * FD, HALF), BF),
            vm((2, NE, K, HALF), BF),
            vm((SLOTS, ROWS), F32),
            vm((SLOTS, ROWS), BF),
            vm((SLOTS, 128), F32),
            vm((2, 8, 128), F32),
            vm((2, 8, 128), F32),
            vm((NC, 2, 8, 128), F32),
            vm((128, 128), F32),
            vm((PADDED, 128), F32),
            vm((5, SLOTS, 128), F32),
            vm((5, PADDED, 128), F32),
            vm((5, SLOTS, 128), F32),
            vm((2, NC, 8, HALF), BF),
            vm((2, NC, 8, HALF), BF),
            vm((NE, 1, HALF), F32),
            vm((NE, 1, HALF), F32),
            vm((NC, 2, 8, HALF), BF),
            vm((2, 4, 2, 8, 384), F32),
            vm((2, 4, 2, 8, 384), F32),
            vm((2, 4, 2, 8, HALF), BF),
            vm((2, 8, HALF), F32),
            vm((2, NC, 8, HALF), BF),
            vm((NE, 1, HALF), F32),
            vm((NE, 1, HALF), F32),
            vm((2, NC, 2, 8, HALF), BF),
            vm((8, PADDED, 128), F32),
            vm((ROWS, SLOTS), BF),
            dma((8,)),
            dma, dma((4,)), dma, dma,
            dma, dma,
            dma, dma,
            dma, dma((5,)),
            dma, dma((2,)),
            dma((2,)), dma((2,)),
            dma, dma((2,)),
            dma, dma((2, 4)),
            dma, dma((2, 4)),
            dma, dma((2,)),
            dma, dma((2,)),
            dma((2,)), dma((2, 2)),
        ],
        compiler_params=pltpu.CompilerParams(
            collective_id=0, has_side_effects=True, vmem_limit_bytes=50 * 2**20
        ),
        cost_estimate=pl.CostEstimate(flops=1_400_000_000, bytes_accessed=14_000_000, transcendentals=400_000),
        name="soft_moe",
    )
    operands = (tokens.reshape(ROWS, 2 * HALF), slot_params.T, jnp.transpose(up_weight, (0, 2, 1)), down_weight)
    mixed = call(*(pltpu.with_memory_space_constraint(v, pltpu.HBM) for v in operands))
    return mixed.reshape(tokens.shape)


def solution(mesh):
    in_specs = (
        P("expert", "seq", None),
        P(None, "expert"),
        P("expert", None, "seq"),
        P("expert", "seq", None),
    )
    out_specs = P("expert", "seq", None)
    return jax.shard_map(shards, mesh=mesh, in_specs=in_specs, out_specs=out_specs, check_vma=False)
```

```python
import functools

import jax
import jax.numpy as jnp
from jax import lax
from jax.experimental import pallas as pl
from jax.experimental.pallas import tpu as pltpu
from jax.sharding import PartitionSpec as P

MESH = pl.DeviceIdType.MESH
BF = jnp.bfloat16
F32 = jnp.float32
NE = 16
NZ = 8
NC = 8
K = 8
HALF = 640
ROWS = 1024
FD = 160
SLOTS = NE * K
PADDED = SLOTS + 16

EXP_FAR = (
    (1, 4), (1, 3), (1, 5), (0, 4), (1, 2), (1, 6), (0, 3), (0, 5),
    (1, 1), (1, 7), (0, 2), (0, 6), (1, 0), (0, 1), (0, 7),
)
EXP_NEAR = tuple(reversed(EXP_FAR))
CHIP_FAR = ((2, 1), (2, 0), (1, 1), (3, 1), (1, 0), (3, 0), (0, 1))
CHIP_NEAR = tuple(reversed(CHIP_FAR))


def nt(a, b):
    return lax.dot_general(a, b, (((1,), (1,)), ((), ())), preferred_element_type=F32)


def mm(a, b):
    return jnp.dot(a, b, preferred_element_type=F32)


def gelu(v):
    return 0.5 * v * (1.0 + lax.erf(v * 0.7071067811865476))


def kernel(
    tok_hbm, sp_hbm, up_hbm, dn_hbm, out_ref,
    tokh, upv, dnv, tab, lg, wt, xs, stat, pst, cst, fin, ft,
    psend, pown, precv, rs_send, rs_recv, a_send, a_recv, xb,
    px_send, px_recv, ro_send, ro_own, ro_recv, b_send, b_recv, ret, mxs, mw,
    load_sem, tab_s, tab_r, tabf_s, tabf_r, pst_s, pst_r, cst_s, cst_r, pp_s, pp_r,
    rs_s, rs_r, w_s, w_r, a_s, a_r, xg_s, xg_r, px_s, px_r, ro_s, ro_r, b_s, b_r,
    rg_s, rg_r,
):
    s = lax.axis_index("seq")
    e = lax.axis_index("expert")
    chip = lax.div(s, 2)
    h = lax.rem(s, 2)
    o = 1 - h
    y = lax.div(chip, 2)
    x_lo = lax.rem(chip, 2)
    z = lax.div(e, 2)
    x_hi = lax.rem(e, 2)
    sib = (chip * 2 + o, e)
    flipped = y * 2 + 1 - x_lo

    def chip_at(p):
        return lax.rem(y + p[0], 4) * 2 + (1 - x_lo if p[1] else x_lo)

    def chip_from(p):
        return chip_at((4 - p[0], p[1]))

    def chip_dev(p):
        return (chip_at(p) * 2 + h, e)

    def exp_at(i):
        return lax.rem(z + i[1], NZ) * 2 + (1 - x_hi if i[0] else x_hi)

    def exp_dev(i):
        return ((flipped if i[0] else chip) * 2 + h, exp_at(i))

    def cid(p):
        return p[0] * 2 + p[1]

    def eid(i):
        return i[0] * NZ + i[1]

    def place_from(i):
        return i[0] * NZ + (1 - i[1]) % NZ

    def copy(src, dst, ssem, rsem, dev):
        return pltpu.make_async_remote_copy(
            src_ref=src, dst_ref=dst, send_sem=ssem, recv_sem=rsem, device_id=dev, device_id_type=MESH
        )

    def send(src, dst, ssem, rsem, dev):
        copy(src, dst, ssem, rsem, dev).start()

    def sent(ref, ssem):
        copy(ref, ref, ssem, ssem, sib).wait_send()

    def blocks(n):
        return tab.at[0, pl.ds(0, n)]

    def arrived(dst, ssem, rsem):
        copy(dst, dst, ssem, rsem, sib).wait_recv()

    barrier = pltpu.get_barrier_semaphore()
    for i in EXP_FAR:
        pl.semaphore_signal(barrier, inc=1, device_id=exp_dev(i), device_id_type=MESH)
    for p in CHIP_FAR:
        pl.semaphore_signal(barrier, inc=1, device_id=chip_dev(p), device_id_type=MESH)
    for p in CHIP_FAR:
        pl.semaphore_signal(barrier, inc=1, device_id=(chip_at(p) * 2 + o, e), device_id_type=MESH)
    pl.semaphore_signal(barrier, inc=1, device_id=sib, device_id_type=MESH)

    loads = []
    ours = pl.ds(pl.multiple_of(h * HALF, 128), HALF)
    c = pltpu.make_async_copy(sp_hbm.at[:, ours], tab.at[h, 1], load_sem.at[4])
    c.start()
    loads.append(c)
    for half in range(2):
        c = pltpu.make_async_copy(tok_hbm.at[:, pl.ds(half * HALF, HALF)], tokh.at[half], load_sem.at[half])
        c.start()
        loads.append(c)
    units = pl.ds(pl.multiple_of(h * FD, 16), FD)
    their_units = pl.ds(pl.multiple_of(o * FD, 16), FD)
    for n, (src, dst) in enumerate(((up_hbm, upv), (dn_hbm, dnv))):
        c = pltpu.make_async_copy(src.at[:, :, ours], dst.at[:, units], load_sem.at[2 + n])
        c.start()
        loads.append(c)
    fin[...] = jnp.zeros_like(fin)
    px_send[...] = jnp.zeros_like(px_send)
    loads[0].wait()
    pl.semaphore_wait(barrier, NE - 1 + 2 * (NC - 1) + 1)

    for i in EXP_FAR:
        send(tab.at[h, 1], tab.at[h, place_from(i)], tab_s, tab_r.at[place_from(i) // 4], exp_dev(i))
    for g in (0, 2, 1, 3):
        arrived(blocks(4 if g else 3), tab_s, tab_r.at[g])
        four = tab.at[h, pl.ds(4 * g, 4)]
        send(four, four, tabf_s, tabf_r, sib)
    loads[1].wait()
    loads[2].wait()
    half_table = tab[h].astype(F32).reshape(SLOTS, HALF).astype(BF)
    for n in range(4):
        part = pl.ds(n * 256, 256)
        lg[:, part] = nt(half_table, tokh[h, part, :])
    arrived(tab.at[o], tabf_s, tabf_r)
    half_table = tab[o].astype(F32).reshape(SLOTS, HALF).astype(BF)
    for n in range(4):
        part = pl.ds(n * 256, 256)
        lg[:, part] += nt(half_table, tokh[o, part, :])

    lane = lax.broadcasted_iota(jnp.int32, (32, 128), 1)
    for r in range(0, SLOTS, 32):
        part = pl.ds(r, 32)
        v = lg[part, :]
        m = jnp.max(v, axis=1, keepdims=True)
        ex = jnp.exp(v - m)
        l = jnp.sum(ex, axis=1, keepdims=True)
        wt[part, :] = ex.astype(BF)
        xs[part, :] = jnp.where(lane < 64, m, l)
    xt = xs[...].T
    m0 = jnp.broadcast_to(xt[0:1, :], (8, 128))
    l0 = jnp.broadcast_to(xt[64:65, :], (8, 128))
    stat[0] = m0
    stat[1] = l0
    send(stat, pst, pst_s, pst_r, sib)

    for n, w in ((0, 2), (2, 2), (4, 1)):
        sums = mm(wt[...], tokh[o, :, pl.ds(n * 128, w * 128)])
        for q in range(w):
            psend[n + q] = sums[:, q * 128 : q * 128 + 128]
        part = pl.ds(n, w)
        send(psend.at[part], precv.at[part], pp_s, pp_r.at[n], sib)
    sums = mm(wt[...], tokh[h])
    all_rows = pl.ds(0, SLOTS)
    for n in range(5):
        pown[n, all_rows, :] = sums[:, n * 128 : n * 128 + 128]
    arrived(pst, pst_s, pst_r)
    m1 = pst[0]
    mc = jnp.maximum(m0, m1)
    g0 = jnp.exp(m0 - mc)
    g1 = jnp.exp(m1 - mc)
    cst[0, 0] = mc
    cst[0, 1] = l0 * g0 + pst[1] * g1
    for p in CHIP_FAR:
        send(cst.at[0], cst.at[cid(p)], cst_s, cst_r, chip_dev(p))
    scale0 = jnp.broadcast_to(g0[0:1, :], (128, 128)).T
    scale1 = jnp.broadcast_to(g1[0:1, :], (128, 128)).T

    def unit(ref, k):
        near = ref[pl.ds(k, NZ, stride=K), :]
        far = ref[pl.ds(NZ * K + k + 1 - 2 * lax.rem(k, 2), NZ, stride=K), :]
        return jnp.concatenate([near[:4], far[:4], near[4:], far[4:]], axis=0)

    def sums_to(g, p):
        j = cid(p)
        send(rs_send.at[g, j], rs_recv.at[g, j], rs_s, rs_r.at[g], chip_dev(p))

    for n, w in ((0, 2), (2, 2), (4, 1)):
        arrived(precv.at[pl.ds(n, w)], pp_s, pp_r.at[n])
        for q in range(n, n + w):
            pown[q, all_rows, :] = pown[q, all_rows, :] * scale0 + precv[q] * scale1
    for p in CHIP_FAR:
        for n in range(5):
            rows = unit(pown.at[n], chip_at(p))
            for g in range(2):
                rs_send[g, cid(p), :, pl.ds(n * 128, 128)] = rows[g * 8 : g * 8 + 8].astype(BF)
        sums_to(1, p)
    for p in CHIP_FAR:
        sums_to(0, p)
    theirs = pl.ds(pl.multiple_of(o * HALF, 128), HALF)
    send(up_hbm.at[:, :, theirs], upv.at[:, units], w_s.at[0], w_r.at[0], sib)
    send(dn_hbm.at[:, :, theirs], dnv.at[:, units], w_s.at[1], w_r.at[1], sib)
    yown = jnp.concatenate([unit(pown.at[n], chip) for n in range(5)], axis=1)

    for n in range(4):
        part = pl.ds(n * 256, 256)
        v = lg[:, part]
        ex = jnp.exp(v - jnp.max(v, axis=0, keepdims=True))
        ex = ex / jnp.sum(ex, axis=0, keepdims=True)
        mxs[2 * n, all_rows, :] = ex[:, :128]
        mxs[2 * n + 1, all_rows, :] = ex[:, 128:]
    for n in range(8):
        part = pl.ds(n * 128, 128)
        rows = []
        for k in range(K):
            near = mxs[n, pl.ds(k, NZ, stride=K), :]
            far = mxs[n, pl.ds(NZ * K + k, NZ, stride=K), :]
            rows += [near[:4], far[:4], near[4:], far[4:]]
        mw[part, :] = jnp.concatenate(rows, axis=0).T.astype(BF)

    sent(blocks(NE - 1), tab_s)
    sent(tab.at[h], tabf_s)
    sent(stat, pst_s)

    arrived(cst.at[pl.ds(1, NC - 1)], cst_s, cst_r)
    top = cst[0, 0]
    for j in range(1, NC):
        top = jnp.maximum(top, cst[j, 0])
    total = jnp.zeros((8, 128), F32)
    for j in range(NC):
        total += cst[j, 1] * jnp.exp(cst[j, 0] - top)
    row = lax.broadcasted_iota(jnp.int32, (8, 128), 0)
    factors = jnp.zeros((8, 128), F32)
    for j in range(NC):
        factors = jnp.where(row == j, jnp.exp(cst[j, 0] - top) / total, factors)
    fin[0:8, :] = factors
    ft[all_rows, :] = fin[...].T
    fk = unit(ft, chip)

    batch = lax.div(z, 4)
    place = batch * 8 + lax.rem(z, 4)
    for g in (1, 0):
        rows = slice(g * 8, g * 8 + 8)
        acc = yown[rows] * fk[rows, 0:1]
        arrived(rs_recv.at[g, pl.ds(1, NC - 1)], rs_s, rs_r.at[g])
        for j in range(1, NC):
            acc += rs_recv[g, j].astype(F32) * fk[rows, j : j + 1]
        a_send[pl.ds(g * 8, 8)] = acc.reshape(8, 1, HALF)
        for i in EXP_FAR:
            u = (i[1] + 1) % NZ
            if u // 4 == g:
                src = a_send.at[g * 8 + i[0] * 4 + u % 4]
                there = place + 4 * i[0]
                send(src, a_recv.at[there], a_s, a_r.at[batch], exp_dev(i))
    a_recv[place] = a_send[1]
    sent(psend, pp_s)
    sent(cst.at[pl.ds(1, NC - 1)], cst_s)
    for c in loads[3:]:
        c.wait()
    arrived(upv.at[:, their_units], w_s.at[0], w_r.at[0])
    arrived(dnv.at[:, their_units], w_s.at[1], w_r.at[1])

    def rows_in(b):
        for others, here in ((7, batch == b), (8, batch != b)):
            wait = functools.partial(arrived, a_recv.at[pl.ds(b * 8, others)], a_s, a_r.at[b])
            pl.when(here)(wait)
        xb[chip, b] = a_recv[pl.ds(b * 8, 8)].reshape(8, HALF).astype(BF)
        for p in CHIP_FAR:
            send(xb.at[chip, b], xb.at[chip, b], xg_s, xg_r.at[b, p[0]], chip_dev(p))

    def first(b, q):
        arrived(blocks(2 if q else 1), xg_s, xg_r.at[b, q])
        for n in range(2):
            k = chip_from((q, n))
            px_send[b, q, n, :, pl.ds(0, 2 * FD)] = nt(xb[k, b], upv[k])
        send(px_send.at[b, q], px_recv.at[b, q], px_s, px_r.at[b, q], sib)

    row8 = lax.broadcasted_iota(jnp.int32, (8, HALF), 0)

    def second(b, q):
        arrived(px_recv.at[b, q], px_s, px_r.at[b, q])
        both = []
        for n in range(2):
            k = chip_from((q, n))
            inner = px_send[b, q, n, :, pl.ds(0, 2 * FD)] + px_recv[b, q, n, :, pl.ds(0, 2 * FD)]
            both.append(mm(gelu(inner).astype(BF), dnv[k]))
        for n in range(2):
            value = jnp.where(row8 < 4, both[n], both[1 - n])
            if q or n:
                ro_send[b, q, n] = value.astype(BF)
                p = (4 - q if q else 0, n)
                sems = ro_s, ro_r.at[b]
                send(ro_send.at[b, q, n], ro_recv.at[b, cid(p)], *sems, chip_dev(p))
            else:
                ro_own[b] = value

    def rows_out(b):
        total_b = ro_own[b]
        arrived(ro_recv.at[b, pl.ds(1, NC - 1)], ro_s, ro_r.at[b])
        for j in range(1, NC):
            total_b += ro_recv[b, j].astype(F32)
        b_send[pl.ds(b * 8, 8)] = total_b.reshape(8, 1, HALF)
        for turn in range(4):
            for rel in (1, 0):
                to_z = b * 4 + turn
                src = b_send.at[b * 8 + rel * 4 + turn]
                dev = ((flipped if rel else chip) * 2 + h, to_z * 2 + (1 - x_hi if rel else x_hi))
                u = lax.rem(z - to_z + 9, NZ)
                there = lax.div(u, 4) * 8 + rel * 4 + lax.rem(u, 4)
                c = copy(src, b_recv.at[there], b_s, b_r.at[lax.div(u, 4)], dev)
                if rel:
                    c.start()
                else:
                    pl.when(z != to_z)(c.start)
        here = b * 8 + lax.rem(z, 4)

        @pl.when(batch == b)
        def _():
            b_recv[1] = b_send[here]

    def result_copies(g):
        mine = ret.at[h, chip, g]
        for target in [c * 2 + core for c in range(NC) for core in (1, 0)]:
            yield copy(mine, mine, rg_s.at[g], rg_r.at[g, h], (target, e)), target

    def results(g):
        for c, target in result_copies(g):
            pl.when(target != s)(c.start)

    def own_clip(g):
        arrived(b_recv.at[pl.ds(g * 8, 7 + g)], b_s, b_r.at[g])
        ret[h, chip, g] = b_recv[pl.ds(g * 8, 8)].reshape(8, HALF).astype(BF)
        results(g)

    rows_in(0)
    rows_in(1)
    for q in (0, 1, 3, 2):
        first(0, q)
    for q in (0, 1, 3, 2):
        second(0, q)
    for q in (0, 1, 3, 2):
        first(1, q)
    for q in (0, 1, 3, 2):
        second(1, q)
    rows_out(0)
    rows_out(1)
    own_clip(0)
    own_clip(1)
    sent(blocks(2 * NC - 2), rs_s)
    sent(a_recv.at[pl.ds(0, NE - 1)], a_s)
    sent(blocks(2 * NC - 2), xg_s)
    sent(upv.at[:, units], w_s.at[0])
    sent(dnv.at[:, units], w_s.at[1])
    sent(px_send, px_s)
    sent(blocks(2 * NC - 2), ro_s)
    sent(b_recv.at[pl.ds(0, NE - 1)], b_s)
    for g in range(2):
        arrived(blocks(NC - 1), rg_s.at[g], rg_r.at[g, h])

    def mix(half):
        table = ret[half].astype(F32).reshape(SLOTS, HALF).astype(BF)
        lanes = pl.ds(pl.multiple_of(half * HALF, 128), HALF)
        for n in range(4):
            part = pl.ds(n * 256, 256)
            out_ref[part, lanes] = mm(mw[part, :], table).astype(BF)

    mix(h)
    for g in range(2):
        arrived(blocks(NC), rg_s.at[g], rg_r.at[g, o])
    mix(o)
    for g in range(2):
        sent(blocks(2 * NC - 1), rg_s.at[g])


def shards(tokens, slot_params, up_weight, down_weight):
    vm = pltpu.VMEM
    dma = pltpu.SemaphoreType.DMA
    call = pl.pallas_call(
        kernel,
        out_shape=jax.ShapeDtypeStruct((ROWS, 2 * HALF), BF),
        in_specs=[pl.BlockSpec(memory_space=pltpu.HBM)] * 4,
        out_specs=pl.BlockSpec(memory_space=pltpu.VMEM),
        scratch_shapes=[
            vm((2, ROWS, HALF), BF),
            vm((K, 2 * FD, HALF), BF),
            vm((K, 2 * FD, HALF), BF),
            vm((2, NE, K, HALF), BF),
            vm((SLOTS, ROWS), F32),
            vm((SLOTS, ROWS), BF),
            vm((SLOTS, 128), F32),
            vm((2, 8, 128), F32),
            vm((2, 8, 128), F32),
            vm((NC, 2, 8, 128), F32),
            vm((128, 128), F32),
            vm((PADDED, 128), F32),
            vm((5, SLOTS, 128), F32),
            vm((5, PADDED, 128), F32),
            vm((5, SLOTS, 128), F32),
            vm((2, NC, 8, HALF), BF),
            vm((2, NC, 8, HALF), BF),
            vm((NE, 1, HALF), F32),
            vm((NE, 1, HALF), F32),
            vm((NC, 2, 8, HALF), BF),
            vm((2, 4, 2, 8, 384), F32),
            vm((2, 4, 2, 8, 384), F32),
            vm((2, 4, 2, 8, HALF), BF),
            vm((2, 8, HALF), F32),
            vm((2, NC, 8, HALF), BF),
            vm((NE, 1, HALF), F32),
            vm((NE, 1, HALF), F32),
            vm((2, NC, 2, 8, HALF), BF),
            vm((8, PADDED, 128), F32),
            vm((ROWS, SLOTS), BF),
            dma((8,)),
            dma, dma((4,)), dma, dma,
            dma, dma,
            dma, dma,
            dma, dma((5,)),
            dma, dma((2,)),
            dma((2,)), dma((2,)),
            dma, dma((2,)),
            dma, dma((2, 4)),
            dma, dma((2, 4)),
            dma, dma((2,)),
            dma, dma((2,)),
            dma((2,)), dma((2, 2)),
        ],
        compiler_params=pltpu.CompilerParams(
            collective_id=0, has_side_effects=True, vmem_limit_bytes=50 * 2**20
        ),
        cost_estimate=pl.CostEstimate(flops=1_400_000_000, bytes_accessed=14_000_000, transcendentals=400_000),
        name="soft_moe",
    )
    operands = (tokens.reshape(ROWS, 2 * HALF), slot_params.T, jnp.transpose(up_weight, (0, 2, 1)), down_weight)
    mixed = call(*(pltpu.with_memory_space_constraint(v, pltpu.HBM) for v in operands))
    return mixed.reshape(tokens.shape)


def solution(mesh):
    in_specs = (
        P("expert", "seq", None),
        P(None, "expert"),
        P("expert", None, "seq"),
        P("expert", "seq", None),
    )
    out_specs = P("expert", "seq", None)
    return jax.shard_map(shards, mesh=mesh, in_specs=in_specs, out_specs=out_specs, check_vma=False)
```
